512 devices in a mesh: rep: 16 (over z), ep: 32 (over y, x, core).
Axes of the slice: x: 4, y: 4, z: 16, core: 2. Of those that a mesh axis runs over, the one named last changes fastest.
Arguments:
- tokens: bfloat16 [2048, 4096], P('rep'), may hold values from -6 to 6
- routes: int32 [2048, 2], P('rep'), may hold values from 0 to 7, all different within a row; in each aligned block of 128 rows (0 to 127, 128 to 255, ...) at most 64 rows name the same one
- gates: bfloat16 [2048, 2], P('rep'), may hold values from 0.19921875 to 1
- w_gate: bfloat16 [32, 1792, 4096], P('ep', 'rep'), may hold values from -0.09375 to 0.09375
- w_up: bfloat16 [32, 1792, 4096], P('ep', 'rep'), may hold values from -0.09375 to 0.09375
- direction: bfloat16 [32, 1792, 4096], P('ep', None, 'rep'), may hold values from -32 to 32
Outputs:
- next_direction: bfloat16 [32, 1792, 4096], P('ep', None, 'rep')
- rayleigh: float32 [1], replicated
The draws below stay inside these ranges and needn't reach their ends.
Inputs may be any that keep to these rules, and one draw needn't show every extreme that they name: `routes`: each row names two different experts. In each aligned block of 128 rows (the tokens of one replica) no expert is named by more than 64 rows, and in some block some expert is named by exactly 64 rows.
All inputs are finite; a program needn't handle non-finite values.
Results may differ from the reference program's by a relative error of at most 0.007.
Values may be sent and summed in bfloat16 or wider, within the bound.
A program may use at most 64 MiB of HBM per device.

```python
import math
import jax
import jax.numpy as jnp
import numpy as np
from jax import lax

D = 4096
FF = 7168
EXPERTS = 8
TOK_REP = 128
ITERS = 2
CAP = 64
SLICES = 4
TOKENS = 2048
N_REP = 16


def draw_direction(key, part):
    key = jax.random.fold_in(key, 11)
    first, second, third = jax.random.split(key, 3)
    rows = EXPERTS * FF
    values = jax.random.normal(first, (rows, D), jnp.float32)
    rising = 3.0
    row_scale = jnp.exp(jax.random.uniform(second, (rows, 1), jnp.float32) * math.log(10.0))
    column = jnp.arange(D, dtype=jnp.float32) / max(D - 1, 1)
    col_scale = jnp.exp(jax.random.uniform(third, (1, D), jnp.float32) * math.log(10.0)) * rising ** column[None, :]
    full = jnp.clip(values * row_scale * col_scale / 4.0, -32.0, 32.0)
    return full.reshape(EXPERTS * SLICES, FF // SLICES, D).astype(jnp.bfloat16)


def steps_of(key, shape, cuts, low, top_value):
    level, own = 1.0, jax.random.fold_in(key, 6)
    for axis_at, parts in cuts:
        heights = jnp.exp(jax.random.uniform(jax.random.fold_in(own, axis_at), (parts,), jnp.float32, low / len(cuts), top_value / len(cuts)))
        level = level * jnp.repeat(heights, shape[axis_at] // parts).reshape([-1 if axis == axis_at else 1 for axis in range(len(shape))])
    return level


def shared_out(rng, own, number, rows, count, top, bound, slope):
    ranking = jax.random.permutation(rng, count)
    heavy_load, common = shares(count, rows * top, bound, slope, True), shares(count, rows * top, bound, slope, False)
    places = jnp.arange(count)

    def named(lengths, offset_by):
        used = int((lengths > 0).sum())
        fixed = max(1, used // 4)
        passed = fixed + (places - fixed + offset_by * (used - fixed)) % max(1, count - fixed)
        return jnp.zeros((count,), jnp.int32).at[ranking[jnp.where(places < fixed, places, passed)]].set(jnp.asarray(lengths, jnp.int32))

    lengths = jnp.where(number % 4 == 0, named(heavy_load, number // 4), named(common, number - number // 4 - 1))
    mixed = jax.random.permutation(jax.random.fold_in(own, 3), count)
    giver, sink = mixed[0:count // 2 * 2:2], mixed[1:count // 2 * 2:2]
    slack = jnp.minimum(lengths[giver] - 1, bound - lengths[sink]) // 2
    slack = jnp.where((giver == ranking[0]) | (sink == ranking[0]) | (lengths[sink] == 0), 0, jnp.maximum(slack, 0))
    passed = jax.random.randint(jax.random.fold_in(own, 4), (count // 2,), 0, 1 << 20) % (slack + 1)
    lengths = lengths.at[giver].add(-passed).at[sink].add(passed)
    members = jnp.searchsorted(jnp.cumsum(lengths), jnp.arange(rows * top), side="right").astype(jnp.int32)
    listing = members.reshape(top, rows).T
    listing = listing[jax.random.permutation(jax.random.fold_in(own, 1), rows)]
    offset_by = jax.random.randint(jax.random.fold_in(own, 2), (rows, 1), 0, top)
    return jnp.take_along_axis(listing, (jnp.arange(top)[None, :] + offset_by) % top, axis=1)


def shares(amount, total, most, skew, full):
    loads = [(1 << 20) // math.isqrt(rank ** skew) + 1 for rank in range(1, amount + 1)]
    largest = most if full else min(most, max(-(-total // amount), total * loads[0] // sum(loads)))
    least = 1 if total - largest >= amount - 1 else 0
    holding, rest = [largest] + [least] * (amount - 1), total - largest - least * (amount - 1)
    while rest > 0:
        free = [i for i in range(1, amount) if holding[i] < largest] or [i for i in range(1, amount) if holding[i] < most]
        pool, left = sum([loads[i] for i in free]), rest
        for i in free:
            extra = min(most - holding[i], max(1, left * loads[i] // pool), rest)
            holding[i] = holding[i] + extra
            rest = rest - extra
    return np.array(holding)


def scatter_about(rng, dims, scale, limit, cuts=(), kind=jnp.bfloat16):
    factor_of = steps_of(rng, dims, cuts, -0.22, 0.18) if cuts else 1.0
    values = jax.random.normal(rng, dims, jnp.float32) * scale * factor_of
    return jnp.minimum(jnp.maximum(values, -limit), limit).astype(kind)


def setup_inputs(seed: int = 0) -> dict:
    seeds = jax.random.split(jax.random.key(seed), 7)
    tokens = scatter_about(seeds[0], (TOKENS, D), 1.0, 6.0, ((0, 16),))
    routes_keys = jax.random.split(jax.random.fold_in(seeds[1], 1), TOKENS // TOK_REP)
    routes_turns = jax.random.permutation(jax.random.fold_in(seeds[1], 3), TOKENS // TOK_REP)
    routes = jax.vmap(lambda own, number: shared_out(jax.random.fold_in(seeds[1], 2), own, number, TOK_REP, EXPERTS, 2, CAP, 2))(routes_keys, routes_turns).reshape((TOKENS, 2))
    gates = jnp.clip(0.19921875 + 0.80078125 * jax.random.uniform(seeds[2], (TOKENS, 2), jnp.float32) ** steps_of(seeds[2], (TOKENS, 2), ((0, 16),), -0.2, 0.2), 0.19921875, 1.0).astype(jnp.bfloat16)
    w_gate = scatter_about(seeds[3], (EXPERTS * SLICES, FF // SLICES, D), D ** -0.5, 0.09375, ((0, 32), (1, 16)))
    w_up = scatter_about(seeds[4], (EXPERTS * SLICES, FF // SLICES, D), D ** -0.5, 0.09375, ((0, 32), (1, 16)))
    direction = draw_direction(jax.random.fold_in(seeds[6], 71), 0)
    return {"tokens": tokens, "routes": routes, "gates": gates, "w_gate": w_gate, "w_up": w_up, "direction": direction}


def reference(tokens, routes, gates, w_gate, w_up, direction):
    rows_cap = N_REP * CAP
    gate_mats = w_gate.reshape(EXPERTS, FF, D)
    up_mats = w_up.reshape(EXPERTS, FF, D)

    def expert_rows(item):
        expert, gate_mat, up_mat = item
        hits = routes == expert
        chosen = jnp.any(hits, axis=1)
        index = jnp.nonzero(chosen, size=rows_cap, fill_value=0)[0].astype(jnp.int32)
        valid = (jnp.arange(rows_cap) < jnp.sum(chosen.astype(jnp.int32))).astype(jnp.float32)
        weight = lax.optimization_barrier(jnp.sum(jnp.where(hits, gates.astype(jnp.float32), 0.0), axis=1))[index] * valid
        picked = tokens[index]
        pre_gate = jnp.dot(picked, gate_mat.T, preferred_element_type=jnp.float32)
        pre_up = jnp.dot(picked, up_mat.T, preferred_element_type=jnp.float32)
        gated = (jax.nn.silu(pre_gate) * pre_up * weight[:, None]).astype(jnp.bfloat16)
        return (gated, index)
    experts_idx = jnp.arange(EXPERTS, dtype=jnp.int32)
    gated_all, index_all = lax.map(expert_rows, (experts_idx, gate_mats, up_mats))
    current = direction.reshape(EXPERTS, FF, D)
    count = float(EXPERTS * FF * D)
    rayleigh = jnp.zeros((), jnp.float32)
    for step in range(ITERS):

        def add_expert(total, item):
            gated, index, block = item
            return (total.at[index].add(jnp.dot(gated, block, preferred_element_type=jnp.float32)), None)
        tangent, unused = lax.scan(add_expert, jnp.zeros((TOKENS, D), jnp.float32), (gated_all, index_all, current))
        sent = tangent.astype(jnp.bfloat16)

        def outer(item):
            gated, index = item
            return jnp.dot(gated.T, sent[index], preferred_element_type=jnp.float32) / N_REP
        product = lax.map(outer, (gated_all, index_all))
        current_f = current.astype(jnp.float32)
        cross = jnp.sum(current_f * product)
        square = jnp.sum(current_f * current_f)
        energy = jnp.sum(product * product)
        rayleigh = cross / count / (square / count + 1e-06)
        current = (product * lax.rsqrt(energy / count + 1e-06)).astype(jnp.bfloat16)
    return (current.reshape(EXPERTS * SLICES, FF // SLICES, D), rayleigh.reshape(1))
```

```python
import functools

import jax
import jax.numpy as jnp
from jax import lax
from jax.experimental import pallas as pl
from jax.experimental.pallas import tpu as pltpu
from jax.sharding import PartitionSpec as P

EXPERTS = 8
CAP = 64
ITERS = 2
LANES = 128
PARTS = 2
F32, BF16 = jnp.float32, jnp.bfloat16


def dot(a, b):
    return jnp.dot(a, b, preferred_element_type=F32)


def dot_nt(a, b):
    return lax.dot_general(a, b, (((1,), (1,)), ((), ())), preferred_element_type=F32)


def active(way, step, part, half):
    if step < half:
        return True
    return (part < PARTS // 2) == (way == 0)


def kernel(
    n_rep, n_ep, units, count,
    rg_ref, tok_ref, wg_ref, wu_ref, dir_ref,
    out_ref, ray_ref,
    wcat, cur0, cur1, rows, rgbuf, hid, hid_t, table, table_t,
    part, swap, snd, rcv, picks, arr, prod,
    red_own, red_sib, red_zsrc, red_z, red_psrc, red_p,
    load_sem, rg_sem, row_sem, sib_sem, hid_sem, swap_sem, a2a_sem, back_sem, fwd_sem,
    rsib_sem, rz_sem, rp_sem,
):
    z = lax.axis_index("rep")
    ep = lax.axis_index("ep")
    chips = n_ep // 2
    per_expert = chips // EXPERTS
    chip, core = ep // 2, lax.rem(ep, 2)
    expert = chip // per_expert
    half = n_rep // 2
    slots = n_rep * CAP
    tok = tok_ref.shape[0]
    width = tok_ref.shape[1] // 2
    piece = width // PARTS
    hpiece = slots // PARTS
    tile = min(256, slots)
    tiles = slots // tile
    sib = {"ep": chip * 2 + 1 - core}
    own_lanes = pl.ds(pl.multiple_of(core * LANES, LANES), LANES)
    other_lanes = pl.ds(pl.multiple_of((1 - core) * LANES, LANES), LANES)

    def remote(src, dst, sems, index, arrive, device):
        return pltpu.make_async_remote_copy(
            src_ref=src, dst_ref=dst,
            send_sem=sems.at[(0, *index)], recv_sem=sems.at[(1, *arrive)],
            device_id=device, device_id_type=pl.DeviceIdType.MESH,
        )

    barrier = pltpu.get_barrier_semaphore()

    @pl.loop(1, n_rep)
    def _(k):
        pl.semaphore_signal(
            barrier, inc=1, device_id={"rep": lax.rem(z + k, n_rep)},
            device_id_type=pl.DeviceIdType.MESH,
        )

    @pl.loop(1, chips)
    def _(k):
        pl.semaphore_signal(
            barrier, inc=1, device_id={"ep": lax.rem(chip + k, chips) * 2 + core},
            device_id_type=pl.DeviceIdType.MESH,
        )

    pl.semaphore_signal(barrier, inc=1, device_id=sib, device_id_type=pl.DeviceIdType.MESH)

    loads = [
        pltpu.make_async_copy(wg_ref, wcat.at[pl.ds(0, units)], load_sem.at[0]),
        pltpu.make_async_copy(wu_ref, wcat.at[pl.ds(LANES, units)], load_sem.at[1]),
        pltpu.make_async_copy(dir_ref, cur0.at[:, pl.ds(0, units)], load_sem.at[2]),
    ]
    for load in loads:
        load.start()
    pad = LANES - units
    wcat[units:LANES, :] = jnp.zeros((pad, wcat.shape[1]), BF16)
    wcat[LANES + units : 2 * LANES, :] = jnp.zeros((pad, wcat.shape[1]), BF16)
    cur0[:, units:LANES, :] = jnp.zeros((n_rep, pad, cur0.shape[2]), BF16)
    hid[:, units:LANES, :] = jnp.zeros((n_rep, pad, slots), BF16)

    before = (
        lax.broadcasted_iota(jnp.int32, (tok, tok), 0)
        < lax.broadcasted_iota(jnp.int32, (tok, tok), 1)
    ).astype(BF16)
    slot_of = lax.broadcasted_iota(jnp.int32, (CAP, tok), 0).astype(F32)

    def slot_table(rg, which):
        hit = jnp.where((rg[0:1] == which) | (rg[1:2] == which), 1.0, 0.0)
        rank = dot(jnp.broadcast_to(hit, (16, tok)).astype(BF16), before)[0:1]
        return jnp.where(slot_of == rank, 1.0, 0.0) * hit

    expert_f = expert.astype(F32)
    own_rg = rg_ref[...]
    own_table = slot_table(own_rg, expert_f).astype(BF16)
    rgbuf[z] = own_rg
    step_w = min(512, width)
    for h in range(2):
        for k in range(width // step_w):
            at = h * width + k * step_w
            rows[h, z, :, k * step_w : (k + 1) * step_w] = dot(
                own_table, tok_ref[:, at : at + step_w]
            ).astype(BF16)

    pl.semaphore_wait(barrier, n_rep - 1 + chips - 1 + 1)

    def block_at(way, step):
        return lax.rem(z + (n_rep - step if way == 0 else step), n_rep)

    def toward(way):
        return {"rep": lax.rem(z + (1 if way == 0 else n_rep - 1), n_rep)}

    def row_copy(way, step, q):
        ref = rows.at[core, block_at(way, step - 1), :, pl.ds(q * piece, piece)]
        i = (way, step - 1, q)
        return remote(ref, ref, row_sem, i, i, toward(way))

    def row_arrival(way, step, q):
        ref = rows.at[core, block_at(way, step), :, pl.ds(q * piece, piece)]
        i = (way, step - 1, q)
        return remote(ref, ref, row_sem, i, i, toward(way))

    def sib_copy(way, step, q):
        ref = rows.at[core, block_at(way, step), :, pl.ds(q * piece, piece)]
        i = (way, step - 1, q)
        return remote(ref, ref, sib_sem, i, i, sib)

    def sib_arrival(way, step, q):
        ref = rows.at[1 - core, block_at(way, step), :, pl.ds(q * piece, piece)]
        i = (way, step - 1, q)
        return remote(ref, ref, sib_sem, i, i, sib)

    order = [
        (step, q, way)
        for step in range(1, half + 1)
        for q in range(PARTS)
        for way in range(2)
        if active(way, step, q, half)
    ]
    for step, q, way in order:
        if step == 1:
            row_copy(way, 1, q).start()

    def rg_copy(k):
        return remote(
            rg_ref, rgbuf.at[z], rg_sem, (lax.rem(z + k, n_rep),), (z,),
            {"rep": lax.rem(z + k, n_rep)},
        )

    def rg_arrival(k):
        b = lax.rem(z + k, n_rep)
        return remote(rg_ref, rgbuf.at[b], rg_sem, (b,), (b,), {"rep": b})

    @pl.loop(1, n_rep)
    def _(k):
        rg_copy(k).start()

    for step, q, way in order:
        row_arrival(way, step, q).wait_recv()
        if step < half and active(way, step + 1, q, half):
            row_copy(way, step + 1, q).start()
        sib_copy(way, step, q).start()
        if (step, q, way) == (1, 0, 0):

            @pl.loop(1, n_rep)
            def _(k):
                rg_arrival(k).wait_recv()

            owned = rgbuf[chip]
            for e in range(EXPERTS):
                t = slot_table(owned, jnp.float32(e))
                table_t[e * CAP : (e + 1) * CAP, :] = t.astype(BF16)
                tt = jnp.transpose(t, (1, 0))
                table[e] = jnp.concatenate([tt] * per_expert, axis=1).astype(BF16)
            for load in loads:
                load.wait()

    for step, q, way in order:
        sib_arrival(way, step, q).wait_recv()

    def hid_copy(way, step, q):
        ref = hid.at[block_at(way, step - 1), pl.ds(0, units), pl.ds(q * hpiece, hpiece)]
        i = (way, step - 1, q)
        return remote(ref, ref, hid_sem, i, i, toward(way))

    def hid_arrival(way, step, q):
        ref = hid.at[block_at(way, step), pl.ds(0, units), pl.ds(q * hpiece, hpiece)]
        i = (way, step - 1, q)
        return remote(ref, ref, hid_sem, i, i, toward(way))

    unit_lanes = pl.ds(pl.multiple_of(z * LANES, LANES), LANES)
    per_tile = tile // CAP
    for m in range(tiles):
        pre = jnp.zeros((tile, 2 * LANES), F32)
        for h in range(2):
            x = rows[h, m * per_tile : (m + 1) * per_tile].reshape(tile, width)
            pre = pre + dot_nt(x, wcat[:, h * width : (h + 1) * width])
        rates = []
        for b in range(m * per_tile, (m + 1) * per_tile):
            rg = rgbuf[b]
            g = jnp.where(rg[0:1] == expert_f, rg[2:3], 0.0) + jnp.where(
                rg[1:2] == expert_f, rg[3:4], 0.0
            )
            rates.append(jnp.sum(slot_table(rg, expert_f) * g, axis=1, keepdims=True))
        rate = jnp.concatenate(rates, axis=0)
        pg, pu = pre[:, :LANES], pre[:, LANES:]
        gated = pg * (1.0 / (1.0 + jnp.exp(-pg))) * pu * rate
        hid_t[m * tile : (m + 1) * tile, unit_lanes] = gated.astype(BF16)
        hid[z, 0:units, m * tile : (m + 1) * tile] = jnp.transpose(gated, (1, 0))[
            :units
        ].astype(BF16)
        if (m + 1) * tile % hpiece == 0:
            q = (m + 1) * tile // hpiece - 1
            for way in range(2):
                if active(way, 1, q, half):
                    hid_copy(way, 1, q).start()
        elif tiles == 1:
            for q in range(PARTS):
                for way in range(2):
                    if active(way, 1, q, half):
                        hid_copy(way, 1, q).start()

    for step, q, way in order:
        hid_arrival(way, step, q).wait_recv()
        if step < half and active(way, step + 1, q, half):
            hid_copy(way, step + 1, q).start()
        b = block_at(way, step)
        lanes = pl.ds(pl.multiple_of(b * LANES, LANES), LANES)
        hid_t[q * hpiece : (q + 1) * hpiece, lanes] = jnp.transpose(
            hid[b, :, q * hpiece : (q + 1) * hpiece], (1, 0)
        )

    def red_sib_copy(it):
        return remote(red_own.at[it], red_sib.at[it], rsib_sem, (it,), (it,), sib)

    def red_z_copy(it, k):
        b = lax.rem(z + k, n_rep)
        return remote(red_zsrc.at[it], red_z.at[it, z], rz_sem, (it, b), (it, z), {"rep": b})

    def red_z_arrival(it, k):
        b = lax.rem(z + k, n_rep)
        return remote(red_zsrc.at[it], red_z.at[it, b], rz_sem, (it, b), (it, b), {"rep": b})

    def red_p_copy(it, k):
        j = lax.rem(chip + k, chips)
        return remote(
            red_psrc.at[it], red_p.at[it, chip], rp_sem, (it, j), (it, chip),
            {"ep": j * 2 + core},
        )

    def red_p_arrival(it, k):
        j = lax.rem(chip + k, chips)
        return remote(
            red_psrc.at[it], red_p.at[it, j], rp_sem, (it, j), (it, j), {"ep": j * 2 + core}
        )

    def reduce_z(it):
        red_sib_copy(it).wait_recv()
        both = red_own[it] + red_sib[it]
        red_zsrc[it] = both
        red_z[it, z] = both

        @pl.loop(1, n_rep)
        def _(k):
            red_z_copy(it, k).start()

    def reduce_plane(it):
        @pl.loop(1, n_rep)
        def _(k):
            red_z_arrival(it, k).wait_recv()

        column = jnp.sum(red_z[it], axis=0)
        red_psrc[it] = column
        red_p[it, chip] = column

        @pl.loop(1, chips)
        def _(k):
            red_p_copy(it, k).start()

    def reduce_end(it):
        @pl.loop(1, chips)
        def _(k):
            red_p_arrival(it, k).wait_recv()

        return jnp.sum(jnp.sum(red_p[it], axis=0), axis=1, keepdims=True)

    row_y, row_x = chip // per_tile, lax.rem(chip, per_tile)

    def tile_at(i):
        return lax.rem(row_y + i, tiles)

    def swap_copy(it, i):
        at = pl.ds(pl.multiple_of(tile_at(i) * tile, tile), tile)
        return remote(
            part.at[it, at, other_lanes], swap.at[it, at], swap_sem, (it, i), (it, i), sib
        )

    def a2a_copy(it, j):
        return remote(
            snd.at[it, j], rcv.at[it, chip], a2a_sem, (it, j), (it, chip),
            {"ep": j * 2 + core},
        )

    def a2a_arrival(it, k):
        j = lax.rem(chip + k, chips)
        return remote(
            snd.at[it, j], rcv.at[it, j], a2a_sem, (it, j), (it, j), {"ep": j * 2 + core}
        )

    def slot_rows(j):
        return pl.ds(pl.multiple_of(j * CAP, CAP), CAP)

    def back_copy(it, k):
        j = lax.rem(chip + k, chips)
        return remote(
            picks.at[it, j // per_expert], arr.at[it, slot_rows(chip), own_lanes],
            back_sem, (it, j), (it, chip), {"ep": j * 2 + core},
        )

    def back_arrival(it, k):
        j = lax.rem(chip + k, chips)
        return remote(
            picks.at[it, j // per_expert], arr.at[it, slot_rows(j), own_lanes],
            back_sem, (it, j), (it, j), {"ep": j * 2 + core},
        )

    def fwd_copy(it, k):
        j = lax.rem(chip + k, chips)
        ref = arr.at[it, slot_rows(j), own_lanes]
        return remote(ref, ref, fwd_sem, (it, j), (it, j), sib)

    def fwd_arrival(it, k):
        j = lax.rem(chip + k, chips)
        ref = arr.at[it, slot_rows(j), other_lanes]
        return remote(ref, ref, fwd_sem, (it, j), (it, j), sib)

    groups = n_rep * LANES // 256
    columns = cur0.shape[2]

    def fold(v):
        s = jnp.sum(v.reshape(v.shape[0] // 8, 8, columns), axis=0)
        return s[:, :LANES] + s[:, LANES:]

    scale = None
    for it in range(ITERS):
        source = cur0 if it == 0 else cur1
        for i in range(tiles):
            at = pl.ds(pl.multiple_of(tile_at(i) * tile, tile), tile)
            part[it, at, :] = dot(
                hid_t[at, :], source[...].reshape(n_rep * LANES, columns)
            )
            swap_copy(it, i).start()
            if it == 1 and i == 0:
                reduce_z(0)
        if it == 1:
            reduce_plane(0)
        for i in range(tiles):
            swap_copy(it, i).wait_recv()
            m = tile_at(i)
            at = pl.ds(pl.multiple_of(m * tile, tile), tile)
            own = (part[it, at, own_lanes] + swap[it, at]).astype(BF16)
            snd[it, pl.ds(m * per_tile, per_tile)] = own.reshape(per_tile, CAP, LANES)
            if i == 0:
                rcv[it, chip] = snd[it, chip]
            for k in range(1 if i == 0 else 0, per_tile):
                a2a_copy(it, m * per_tile + lax.rem(row_x + k, per_tile)).start()

        @pl.loop(1, chips)
        def _(k):
            a2a_arrival(it, k).wait_recv()

        tangent = jnp.zeros((tok, LANES), F32)
        for e in range(EXPERTS):
            got = rcv[it, e * per_expert : (e + 1) * per_expert].reshape(
                per_expert * CAP, LANES
            )
            tangent = tangent + dot(table[e], got)
        if it == 1:
            scale = lax.rsqrt(reduce_end(0)[0:1] / count + 1e-06)
            tangent = tangent * scale
        sent = tangent.astype(BF16)
        picks[it] = dot(table_t[...], sent).astype(BF16).reshape(EXPERTS, CAP, LANES)
        arr[it, slot_rows(chip), own_lanes] = picks[it, expert]
        fwd_copy(it, 0).start()

        @pl.loop(1, chips)
        def _(k):
            back_copy(it, k).start()

        @pl.loop(1, chips)
        def _(k):
            back_arrival(it, k).wait_recv()
            fwd_copy(it, k).start()

        @pl.loop(0, chips)
        def _(k):
            fwd_arrival(it, k).wait_recv()

        energy = jnp.zeros((8, LANES), F32)
        cross, square = energy, energy
        for g in range(groups):
            x = hid[2 * g : 2 * g + 2].reshape(256, slots)
            p = dot(x, arr[it]) / n_rep
            energy = energy + fold(p * p)
            if it == 0:
                cur1[2 * g : 2 * g + 2] = p.astype(BF16).reshape(2, LANES, columns)
            else:
                prod[2 * g : 2 * g + 2] = p.reshape(2, LANES, columns)
                c = cur1[2 * g : 2 * g + 2].reshape(256, columns).astype(F32) * scale
                cross = cross + fold(c * p)
                square = square + fold(c * c)
        red_own[it] = jnp.concatenate(
            [jnp.sum(v, axis=0, keepdims=True) for v in (energy, cross, square)]
            + [jnp.zeros((5, LANES), F32)],
            axis=0,
        )
        red_sib_copy(it).start()

    reduce_z(1)
    reduce_plane(1)
    total = reduce_end(1)
    ray_ref[...] = jnp.broadcast_to(
        total[1:2] / count / (total[2:3] / count + 1e-06), (8, LANES)
    )
    last = lax.rsqrt(total[0:1] / count + 1e-06)
    for g in range(n_rep):
        out_ref[g] = (prod[g, :units, :] * last).astype(BF16)

    @pl.loop(1, n_rep)
    def _(k):
        rg_copy(k).wait_send()
        for it in range(ITERS):
            red_z_copy(it, k).wait_send()

    for step, q, way in order:
        row_copy(way, step, q).wait_send()
        sib_copy(way, step, q).wait_send()
        hid_copy(way, step, q).wait_send()
    for it in range(ITERS):
        red_sib_copy(it).wait_send()
        for i in range(tiles):
            swap_copy(it, i).wait_send()

        @pl.loop(1, chips)
        def _(k):
            a2a_copy(it, lax.rem(chip + k, chips)).wait_send()
            back_copy(it, k).wait_send()
            red_p_copy(it, k).wait_send()

        @pl.loop(0, chips)
        def _(k):
            fwd_copy(it, k).wait_send()


def on_device(tokens, routes, gates, w_gate, w_up, direction):
    n_rep = lax.axis_size("rep")
    n_ep = lax.axis_size("ep")
    chips = n_ep // 2
    tok, depth = tokens.shape
    units, inner = w_gate.shape[1], direction.shape[1]
    columns = direction.shape[2]
    slots = n_rep * CAP
    half = n_rep // 2
    width = depth // 2
    count = float(n_rep * n_ep * inner * columns)
    rg = jnp.concatenate(
        [routes.T.astype(F32), gates.T.astype(F32), jnp.zeros((4, tok), F32)], axis=0
    )
    dma = pltpu.SemaphoreType.DMA
    per_expert = chips // EXPERTS
    out, ray = pl.pallas_call(
        functools.partial(kernel, n_rep, n_ep, units, count),
        out_shape=(
            jax.ShapeDtypeStruct((n_rep, units, columns), BF16),
            jax.ShapeDtypeStruct((8, LANES), F32),
        ),
        in_specs=[
            pl.BlockSpec(memory_space=pltpu.VMEM),
            pl.BlockSpec(memory_space=pltpu.VMEM),
            pl.BlockSpec(memory_space=pl.ANY),
            pl.BlockSpec(memory_space=pl.ANY),
            pl.BlockSpec(memory_space=pl.ANY),
        ],
        out_specs=(
            pl.BlockSpec(memory_space=pltpu.VMEM),
            pl.BlockSpec(memory_space=pltpu.VMEM),
        ),
        scratch_shapes=[
            pltpu.VMEM((2 * LANES, depth), BF16),
            pltpu.VMEM((n_rep, LANES, columns), BF16),
            pltpu.VMEM((n_rep, LANES, columns), BF16),
            pltpu.VMEM((2, n_rep, CAP, width), BF16),
            pltpu.VMEM((n_rep, 8, tok), F32),
            pltpu.VMEM((n_rep, LANES, slots), BF16),
            pltpu.VMEM((slots, n_rep * LANES), BF16),
            pltpu.VMEM((EXPERTS, tok, per_expert * CAP), BF16),
            pltpu.VMEM((EXPERTS * CAP, tok), BF16),
            pltpu.VMEM((ITERS, slots, columns), F32),
            pltpu.VMEM((ITERS, slots, LANES), F32),
            pltpu.VMEM((ITERS, chips, CAP, LANES), BF16),
            pltpu.VMEM((ITERS, chips, CAP, LANES), BF16),
            pltpu.VMEM((ITERS, EXPERTS, CAP, LANES), BF16),
            pltpu.VMEM((ITERS, slots, columns), BF16),
            pltpu.VMEM((n_rep, LANES, columns), F32),
            pltpu.VMEM((ITERS, 8, LANES), F32),
            pltpu.VMEM((ITERS, 8, LANES), F32),
            pltpu.VMEM((ITERS, 8, LANES), F32),
            pltpu.VMEM((ITERS, n_rep, 8, LANES), F32),
            pltpu.VMEM((ITERS, 8, LANES), F32),
            pltpu.VMEM((ITERS, chips, 8, LANES), F32),
            dma((3,)),
            dma((2, n_rep)),
            dma((2, 2, half, PARTS)),
            dma((2, 2, half, PARTS)),
            dma((2, 2, half, PARTS)),
            dma((2, ITERS, max(1, slots // 256))),
            dma((2, ITERS, chips)),
            dma((2, ITERS, chips)),
            dma((2, ITERS, chips)),
            dma((2, ITERS)),
            dma((2, ITERS, n_rep)),
            dma((2, ITERS, chips)),
        ],
        compiler_params=pltpu.CompilerParams(
            collective_id=0, has_side_effects=True, vmem_limit_bytes=56 * 2**20
        ),
    )(rg, tokens, w_gate[0], w_up[0], direction[0].reshape(n_rep, units, columns))
    return out.reshape(1, inner, columns), ray[0, :1]


def solution(mesh):
    return jax.shard_map(
        on_device,
        mesh=mesh,
        in_specs=(
            P("rep", None),
            P("rep", None),
            P("rep", None),
            P("ep", "rep", None),
            P("ep", "rep", None),
            P("ep", None, "rep"),
        ),
        out_specs=(P("ep", None, "rep"), P()),
        check_vma=False,
    )
```

```python
import functools

import jax
import jax.numpy as jnp
from jax import lax
from jax.experimental import pallas as pl
from jax.experimental.pallas import tpu as pltpu
from jax.sharding import PartitionSpec as P

EXPERTS = 8
CAP = 64
ITERS = 2
LANES = 128
PARTS = 4
F32, BF16 = jnp.float32, jnp.bfloat16


def dot(a, b):
    return jnp.dot(a, b, preferred_element_type=F32)


def dot_nt(a, b):
    return lax.dot_general(a, b, (((1,), (1,)), ((), ())), preferred_element_type=F32)


def active(way, step, part, half):
    if step < half:
        return True
    return (part < PARTS // 2) == (way == 0)


def kernel(
    n_rep, n_ep, units, count,
    routes_ref, gates_ref, tok_ref, wg_ref, wu_ref, dir_ref,
    out_ref, scale_ref, ray_ref,
    wcat, cur0, cur1, rows, rgbuf, hid, hid_t, table, table_t,
    rates, part, swap, snd, rcv, picks, arr,
    red_own, red_z, red_psrc, red_p,
    load_sem, rg_sem, row_sem, pair_sem, sib_sem, hid_sem, swap_sem, a2a_sem, back_sem, fwd_sem,
    rz_sem, rp_sem,
):
    z = lax.axis_index("rep")
    ep = lax.axis_index("ep")
    chips = n_ep // 2
    per_expert = chips // EXPERTS
    chip, core = ep // 2, lax.rem(ep, 2)
    expert = chip // per_expert
    half = n_rep // 2
    slots = n_rep * CAP
    tok = tok_ref.shape[0]
    width = tok_ref.shape[1] // 2
    third = width // 3 // LANES * LANES
    parity = lax.rem(chip, 2)
    hpiece = slots // PARTS
    tile = min(256, slots)
    tiles = slots // tile
    sib = {"ep": chip * 2 + 1 - core}
    pair = {"ep": (chip + 1 - 2 * parity) * 2 + core}
    own_lanes = pl.ds(pl.multiple_of(core * LANES, LANES), LANES)
    other_lanes = pl.ds(pl.multiple_of((1 - core) * LANES, LANES), LANES)

    def remote(src, dst, sems, index, arrive, device):
        return pltpu.make_async_remote_copy(
            src_ref=src, dst_ref=dst,
            send_sem=sems.at[(0, *index)], recv_sem=sems.at[(1, *arrive)],
            device_id=device, device_id_type=pl.DeviceIdType.MESH,
        )

    barrier = pltpu.get_barrier_semaphore()

    @pl.loop(1, n_rep)
    def _(k):
        pl.semaphore_signal(
            barrier, inc=1, device_id={"rep": lax.rem(z + k, n_rep)},
            device_id_type=pl.DeviceIdType.MESH,
        )

    @pl.loop(1, n_ep)
    def _(k):
        pl.semaphore_signal(
            barrier, inc=1, device_id={"ep": lax.rem(ep + k, n_ep)},
            device_id_type=pl.DeviceIdType.MESH,
        )

    loads = [
        pltpu.make_async_copy(wg_ref, wcat.at[pl.ds(0, units)], load_sem.at[0]),
        pltpu.make_async_copy(wu_ref, wcat.at[pl.ds(LANES, units)], load_sem.at[1]),
        pltpu.make_async_copy(dir_ref, cur0.at[:, pl.ds(0, units)], load_sem.at[2]),
    ]
    for load in loads:
        load.start()
    pad = LANES - units
    wcat[units:LANES, :] = jnp.zeros((pad, wcat.shape[1]), BF16)
    wcat[LANES + units : 2 * LANES, :] = jnp.zeros((pad, wcat.shape[1]), BF16)
    cur0[:, units:LANES, :] = jnp.zeros((n_rep, pad, cur0.shape[2]), BF16)
    hid[:, units:LANES, :] = jnp.zeros((n_rep, pad, slots), BF16)

    before = (
        lax.broadcasted_iota(jnp.int32, (tok, tok), 0)
        < lax.broadcasted_iota(jnp.int32, (tok, tok), 1)
    ).astype(BF16)
    slot_of = lax.broadcasted_iota(jnp.int32, (CAP, tok), 0).astype(F32)

    def slot_table(rg, which):
        hit = jnp.where((rg[0:1] == which) | (rg[1:2] == which), 1.0, 0.0)
        rank = dot(jnp.broadcast_to(hit, (16, tok)).astype(BF16), before)[0:1]
        return jnp.where(slot_of == rank, 1.0, 0.0) * hit

    expert_f = expert.astype(F32)
    own_rg = jnp.concatenate(
        [routes_ref[...].astype(F32), gates_ref[...].astype(F32), jnp.zeros((4, tok), F32)], axis=0
    )
    own_table = slot_table(own_rg, expert_f).astype(BF16)
    rgbuf[z] = own_rg
    step_w = min(512, width)
    for h in range(2):
        for k in range(width // step_w):
            at = h * width + k * step_w
            rows[h, z, :, k * step_w : (k + 1) * step_w] = dot(
                own_table, tok_ref[:, at : at + step_w]
            ).astype(BF16)

    pl.semaphore_wait(barrier, n_rep - 1 + n_ep - 1)

    def block_at(way, step):
        return lax.rem(z + (n_rep - step if way == 0 else step), n_rep)

    def toward(way):
        return {"rep": lax.rem(z + (1 if way == 0 else n_rep - 1), n_rep)}

    def rows_of(q):
        return pl.ds(q % 2 * (CAP // 2), CAP // 2)

    def lanes_of(q):
        if q // 2 == 1:
            return pl.ds(2 * third, width - 2 * third)
        first = parity if q // 2 == 0 else 1 - parity
        return pl.ds(pl.multiple_of(first * third, LANES), third)

    def row_copy(way, step, q):
        ref = rows.at[core, block_at(way, step - 1), rows_of(q), lanes_of(q)]
        i = (way, step - 1, q)
        return remote(ref, ref, row_sem, i, i, toward(way))

    def row_arrival(way, step, q):
        ref = rows.at[core, block_at(way, step), rows_of(q), lanes_of(q)]
        i = (way, step - 1, q)
        return remote(ref, ref, row_sem, i, i, toward(way))

    def pair_copy(way, step, q):
        ref = rows.at[core, block_at(way, step), rows_of(q), lanes_of(q)]
        i = (way, step - 1, q)
        return remote(ref, ref, pair_sem, i, i, pair)

    def pair_arrival(way, step, q):
        ref = rows.at[core, block_at(way, step), rows_of(q), lanes_of(q + 4)]
        i = (way, step - 1, q)
        return remote(ref, ref, pair_sem, i, i, pair)

    def sib_copy(way, step, q):
        ref = rows.at[core, block_at(way, step), rows_of(q), lanes_of(q)]
        i = (way, step - 1, q)
        return remote(ref, ref, sib_sem, i, i, sib)

    def sib_arrival(way, step, q):
        ref = rows.at[1 - core, block_at(way, step), rows_of(q), lanes_of(q)]
        i = (way, step - 1, q)
        return remote(ref, ref, sib_sem, i, i, sib)

    def rg_copy(way, step):
        ref = rgbuf.at[block_at(way, step - 1)]
        i = (way, step - 1)
        return remote(ref, ref, rg_sem, i, i, toward(way))

    def rg_arrival(way, step):
        ref = rgbuf.at[block_at(way, step)]
        i = (way, step - 1)
        return remote(ref, ref, rg_sem, i, i, toward(way))

    order = [
        (step, q, way)
        for step in range(1, half + 1)
        for q in range(PARTS)
        for way in range(2)
        if active(way, step, q, half)
    ]
    passed = [(step, q, way) for step, q, way in order if q < 2]
    whole = [(step, way) for step, q, way in passed if q == 0]
    for way in range(2):
        if active(way, 1, 0, half):
            rg_copy(way, 1).start()
    for step, q, way in order:
        if step == 1:
            row_copy(way, 1, q).start()

    def to_sibling(step, q, way):
        pair_arrival(way, step, q).wait_recv()
        sib_copy(way, step, q + 4).start()

    late = list(passed)
    for step, q, way in order:
        row_arrival(way, step, q).wait_recv()
        if step < half and active(way, step + 1, q, half):
            row_copy(way, step + 1, q).start()
        if q < 2:
            pair_copy(way, step, q).start()
        if q == 0:
            rg_arrival(way, step).wait_recv()
            if step < half and active(way, step + 1, 0, half):
                rg_copy(way, step + 1).start()
        sib_copy(way, step, q).start()
        if q >= 2 and late and late[0][0] < step:
            to_sibling(*late.pop(0))

    for b in range(n_rep):
        rg = rgbuf[b]
        g = jnp.where(rg[0:1] == expert_f, rg[2:3], 0.0) + jnp.where(
            rg[1:2] == expert_f, rg[3:4], 0.0
        )
        rate = jnp.sum(slot_table(rg, expert_f) * g, axis=1, keepdims=True)
        rates[b * CAP : (b + 1) * CAP] = jnp.broadcast_to(rate, (CAP, LANES))
    for load in loads:
        load.wait()
    for step, q, way in late:
        to_sibling(step, q, way)
    for step, q, way in order:
        sib_arrival(way, step, q).wait_recv()
    for step, q, way in passed:
        sib_arrival(way, step, q + 4).wait_recv()

    def hid_copy(way, step, q):
        ref = hid.at[block_at(way, step - 1), pl.ds(0, units), pl.ds(q * hpiece, hpiece)]
        i = (way, step - 1, q)
        return remote(ref, ref, hid_sem, i, i, toward(way))

    def hid_arrival(way, step, q):
        ref = hid.at[block_at(way, step), pl.ds(0, units), pl.ds(q * hpiece, hpiece)]
        i = (way, step - 1, q)
        return remote(ref, ref, hid_sem, i, i, toward(way))

    unit_lanes = pl.ds(pl.multiple_of(z * LANES, LANES), LANES)
    per_tile = tile // CAP
    for m in range(tiles):
        pre = jnp.zeros((tile, 2 * LANES), F32)
        for h in range(2):
            x = rows[h, m * per_tile : (m + 1) * per_tile].reshape(tile, width)
            pre = pre + dot_nt(x, wcat[:, h * width : (h + 1) * width])
        pg, pu = pre[:, :LANES], pre[:, LANES:]
        gated = pg * (1.0 / (1.0 + jnp.exp(-pg))) * pu * rates[m * tile : (m + 1) * tile]
        hid_t[m * tile : (m + 1) * tile, unit_lanes] = gated.astype(BF16)
        hid[z, 0:units, m * tile : (m + 1) * tile] = jnp.transpose(gated, (1, 0))[
            :units
        ].astype(BF16)
        for q in range(m * tile // hpiece, (m + 1) * tile // hpiece):
            for way in range(2):
                if active(way, 1, q, half):
                    hid_copy(way, 1, q).start()

    for step, q, way in order:
        hid_arrival(way, step, q).wait_recv()
        if step < half and active(way, step + 1, q, half):
            hid_copy(way, step + 1, q).start()
        b = block_at(way, step)
        lanes = pl.ds(pl.multiple_of(b * LANES, LANES), LANES)
        hid_t[q * hpiece : (q + 1) * hpiece, lanes] = jnp.transpose(
            hid[b, :, q * hpiece : (q + 1) * hpiece], (1, 0)
        )

    def red_z_copy(it, k):
        b = lax.rem(z + k, n_rep)
        return remote(red_own.at[it], red_z.at[it, z], rz_sem, (it, b), (it, z), {"rep": b})

    def red_z_arrival(it, k):
        b = lax.rem(z + k, n_rep)
        return remote(red_own.at[it], red_z.at[it, b], rz_sem, (it, b), (it, b), {"rep": b})

    def red_p_copy(it, k):
        j = lax.rem(ep + k, n_ep)
        return remote(red_psrc.at[it], red_p.at[it, ep], rp_sem, (it, j), (it, ep), {"ep": j})

    def red_p_arrival(it, k):
        j = lax.rem(ep + k, n_ep)
        return remote(red_psrc.at[it], red_p.at[it, j], rp_sem, (it, j), (it, j), {"ep": j})

    def reduce_z(it):
        red_z[it, z] = red_own[it]

        @pl.loop(1, n_rep)
        def _(k):
            red_z_copy(it, k).start()

    def reduce_plane(it):
        @pl.loop(1, n_rep)
        def _(k):
            red_z_arrival(it, k).wait_recv()

        column = jnp.sum(red_z[it], axis=0)
        red_psrc[it] = column
        red_p[it, ep] = column

        @pl.loop(1, n_ep)
        def _(k):
            red_p_copy(it, k).start()

    def reduce_end(it):
        @pl.loop(1, n_ep)
        def _(k):
            red_p_arrival(it, k).wait_recv()

        return jnp.sum(jnp.sum(red_p[it], axis=0), axis=1, keepdims=True)

    row_y, row_x = chip // per_tile, lax.rem(chip, per_tile)

    def tile_at(i):
        return lax.rem(row_y + i, tiles)

    def swap_copy(it, i):
        at = pl.ds(pl.multiple_of(tile_at(i) * tile, tile), tile)
        return remote(
            part.at[it, at, other_lanes], swap.at[it, at], swap_sem, (it, i), (it, i), sib
        )

    def a2a_copy(it, j):
        return remote(
            snd.at[it, j], rcv.at[it, chip], a2a_sem, (it, j), (it, chip),
            {"ep": j * 2 + core},
        )

    def a2a_arrival(it, k):
        j = lax.rem(chip + k, chips)
        return remote(
            snd.at[it, j], rcv.at[it, j], a2a_sem, (it, j), (it, j), {"ep": j * 2 + core}
        )

    def slot_rows(j):
        return pl.ds(pl.multiple_of(j * CAP, CAP), CAP)

    def back_copy(it, k):
        j = lax.rem(chip + k, chips)
        return remote(
            picks.at[it, j // per_expert], arr.at[it, slot_rows(chip), own_lanes],
            back_sem, (it, j), (it, chip), {"ep": j * 2 + core},
        )

    def back_arrival(it, k):
        j = lax.rem(chip + k, chips)
        return remote(
            picks.at[it, j // per_expert], arr.at[it, slot_rows(j), own_lanes],
            back_sem, (it, j), (it, j), {"ep": j * 2 + core},
        )

    def fwd_copy(it, k):
        j = lax.rem(chip + k, chips)
        ref = arr.at[it, slot_rows(j), own_lanes]
        return remote(ref, ref, fwd_sem, (it, j), (it, j), sib)

    def fwd_arrival(it, k):
        j = lax.rem(chip + k, chips)
        ref = arr.at[it, slot_rows(j), other_lanes]
        return remote(ref, ref, fwd_sem, (it, j), (it, j), sib)

    groups = n_rep * LANES // 256
    columns = cur0.shape[2]

    def fold(v):
        s = jnp.sum(v.reshape(v.shape[0] // 8, 8, columns), axis=0)
        return s[:, :LANES] + s[:, LANES:]

    scale = None
    for it in range(ITERS):
        source = cur0 if it == 0 else cur1
        for i in range(tiles):
            at = pl.ds(pl.multiple_of(tile_at(i) * tile, tile), tile)
            part[it, at, :] = dot(
                hid_t[at, :], source[...].reshape(n_rep * LANES, columns)
            )
            swap_copy(it, i).start()
        for i in range(tiles):
            swap_copy(it, i).wait_recv()
            m = tile_at(i)
            at = pl.ds(pl.multiple_of(m * tile, tile), tile)
            own = (part[it, at, own_lanes] + swap[it, at]).astype(BF16)
            snd[it, pl.ds(m * per_tile, per_tile)] = own.reshape(per_tile, CAP, LANES)
            if i == 0:
                rcv[it, chip] = snd[it, chip]
            for k in range(1 if i == 0 else 0, per_tile):
                a2a_copy(it, m * per_tile + lax.rem(row_x + k, per_tile)).start()

        if it == 0:
            owned = rgbuf[chip]
            for e in range(EXPERTS):
                t = slot_table(owned, jnp.float32(e))
                table_t[e * CAP : (e + 1) * CAP, :] = t.astype(BF16)
                tt = jnp.transpose(t, (1, 0))
                table[e] = jnp.concatenate([tt] * per_expert, axis=1).astype(BF16)

        @pl.loop(1, chips)
        def _(k):
            a2a_arrival(it, k).wait_recv()

        tangent = jnp.zeros((tok, LANES), F32)
        for e in range(EXPERTS):
            got = rcv[it, e * per_expert : (e + 1) * per_expert].reshape(
                per_expert * CAP, LANES
            )
            tangent = tangent + dot(table[e], got)
        sent = tangent.astype(BF16)
        picks[it] = dot(table_t[...], sent).astype(BF16).reshape(EXPERTS, CAP, LANES)
        arr[it, slot_rows(chip), own_lanes] = picks[it, expert]
        fwd_copy(it, 0).start()

        @pl.loop(1, chips)
        def _(k):
            back_copy(it, k).start()

        if it == 1:
            reduce_plane(0)

        @pl.loop(1, chips)
        def _(k):
            back_arrival(it, k).wait_recv()
            fwd_copy(it, k).start()

        rest = 1.0 / n_rep
        if it == 1:
            scale = lax.rsqrt(reduce_end(0)[0:1] / count + 1e-06)
            power = jnp.exp2(jnp.floor(jnp.log2(scale))).astype(BF16)
            rest = scale / power.astype(F32) * rest

        @pl.loop(0, chips)
        def _(k):
            fwd_arrival(it, k).wait_recv()

        moved = arr[it] if it == 0 else arr[it] * power
        energy = jnp.zeros((8, LANES), F32)
        cross, square = energy, energy
        for g in range(groups):
            x = hid[2 * g : 2 * g + 2].reshape(256, slots)
            p = dot(x, moved) * rest
            energy = energy + fold(p * p)
            if it == 0:
                cur1[2 * g : 2 * g + 2] = p.astype(BF16).reshape(2, LANES, columns)
            else:
                out_ref[2 * g : 2 * g + 2] = p.reshape(2, LANES, columns)[:, :units]
                c = cur1[2 * g : 2 * g + 2].reshape(256, columns).astype(F32) * scale
                cross = cross + fold(c * p)
                square = square + fold(c * c)
        red_own[it] = jnp.concatenate(
            [jnp.sum(v, axis=0, keepdims=True) for v in (energy, cross, square)]
            + [jnp.zeros((5, LANES), F32)],
            axis=0,
        )
        reduce_z(it)

    reduce_plane(1)
    total = reduce_end(1)
    ray = total[1:2] / count / (total[2:3] / count + 1e-06)
    ray_ref[0] = jnp.sum(ray)
    scale_ref[0] = jnp.sum(lax.rsqrt(total[0:1] / count + 1e-06))

    @pl.loop(1, n_rep)
    def _(k):
        for it in range(ITERS):
            red_z_copy(it, k).wait_send()

    for step, q, way in order:
        row_copy(way, step, q).wait_send()
        sib_copy(way, step, q).wait_send()
        hid_copy(way, step, q).wait_send()
    for step, way in whole:
        rg_copy(way, step).wait_send()
    for step, q, way in passed:
        pair_copy(way, step, q).wait_send()
        sib_copy(way, step, q + 4).wait_send()
    for it in range(ITERS):
        for i in range(tiles):
            swap_copy(it, i).wait_send()

        @pl.loop(1, chips)
        def _(k):
            a2a_copy(it, lax.rem(chip + k, chips)).wait_send()
            back_copy(it, k).wait_send()

        @pl.loop(1, n_ep)
        def _(k):
            red_p_copy(it, k).wait_send()

        @pl.loop(0, chips)
        def _(k):
            fwd_copy(it, k).wait_send()


def on_device(tokens, routes, gates, w_gate, w_up, direction):
    n_rep = lax.axis_size("rep")
    n_ep = lax.axis_size("ep")
    chips = n_ep // 2
    tok, depth = tokens.shape
    units, inner = w_gate.shape[1], direction.shape[1]
    columns = direction.shape[2]
    slots = n_rep * CAP
    half = n_rep // 2
    width = depth // 2
    count = float(n_rep * n_ep * inner * columns)
    dma = pltpu.SemaphoreType.DMA
    per_expert = chips // EXPERTS
    out, scale, ray = pl.pallas_call(
        functools.partial(kernel, n_rep, n_ep, units, count),
        out_shape=(
            jax.ShapeDtypeStruct((n_rep, units, columns), F32),
            jax.ShapeDtypeStruct((1,), F32),
            jax.ShapeDtypeStruct((1,), F32),
        ),
        in_specs=[
            pl.BlockSpec(memory_space=pltpu.VMEM),
            pl.BlockSpec(memory_space=pltpu.VMEM),
            pl.BlockSpec(memory_space=pltpu.VMEM),
            pl.BlockSpec(memory_space=pl.ANY),
            pl.BlockSpec(memory_space=pl.ANY),
            pl.BlockSpec(memory_space=pl.ANY),
        ],
        out_specs=(
            pl.BlockSpec(memory_space=pltpu.VMEM),
            pl.BlockSpec(memory_space=pltpu.SMEM),
            pl.BlockSpec(memory_space=pltpu.SMEM),
        ),
        scratch_shapes=[
            pltpu.VMEM((2 * LANES, depth), BF16),
            pltpu.VMEM((n_rep, LANES, columns), BF16),
            pltpu.VMEM((n_rep, LANES, columns), BF16),
            pltpu.VMEM((2, n_rep, CAP, width), BF16),
            pltpu.VMEM((n_rep, 8, tok), F32),
            pltpu.VMEM((n_rep, LANES, slots), BF16),
            pltpu.VMEM((slots, n_rep * LANES), BF16),
            pltpu.VMEM((EXPERTS, tok, per_expert * CAP), BF16),
            pltpu.VMEM((EXPERTS * CAP, tok), BF16),
            pltpu.VMEM((slots, LANES), F32),
            pltpu.VMEM((ITERS, slots, columns), F32),
            pltpu.VMEM((ITERS, slots, LANES), F32),
            pltpu.VMEM((ITERS, chips, CAP, LANES), BF16),
            pltpu.VMEM((ITERS, chips, CAP, LANES), BF16),
            pltpu.VMEM((ITERS, EXPERTS, CAP, LANES), BF16),
            pltpu.VMEM((ITERS, slots, columns), BF16),
            pltpu.VMEM((ITERS, 8, LANES), F32),
            pltpu.VMEM((ITERS, n_rep, 8, LANES), F32),
            pltpu.VMEM((ITERS, 8, LANES), F32),
            pltpu.VMEM((ITERS, n_ep, 8, LANES), F32),
            dma((3,)),
            dma((2, 2, half)),
            dma((2, 2, half, PARTS)),
            dma((2, 2, half, 2)),
            dma((2, 2, half, PARTS + 2)),
            dma((2, 2, half, PARTS)),
            dma((2, ITERS, max(1, slots // 256))),
            dma((2, ITERS, chips)),
            dma((2, ITERS, chips)),
            dma((2, ITERS, chips)),
            dma((2, ITERS, n_rep)),
            dma((2, ITERS, n_ep)),
        ],
        compiler_params=pltpu.CompilerParams(
            collective_id=0, has_side_effects=True, vmem_limit_bytes=56 * 2**20
        ),
    )(routes.T, gates.T, tokens, w_gate[0], w_up[0], direction[0].reshape(n_rep, units, columns))
    return (out * scale[0]).astype(BF16).reshape(1, inner, columns), ray


def solution(mesh):
    return jax.shard_map(
        on_device,
        mesh=mesh,
        in_specs=(
            P("rep", None),
            P("rep", None),
            P("rep", None),
            P("ep", "rep", None),
            P("ep", "rep", None),
            P("ep", None, "rep"),
        ),
        out_specs=(P("ep", None, "rep"), P()),
        check_vma=False,
    )
```

```python
import functools
import math

import jax
import jax.numpy as jnp
from jax import lax
from jax.experimental import pallas as pl
from jax.experimental.pallas import tpu as pltpu
from jax.sharding import PartitionSpec as P

EXPERTS = 8
CAP = 64
ITERS = 2
LANES = 128
PARTS = 4
F32, BF16 = jnp.float32, jnp.bfloat16


def dot(a, b):
    return jnp.dot(a, b, preferred_element_type=F32)


def dot_nt(a, b):
    return lax.dot_general(a, b, (((1,), (1,)), ((), ())), preferred_element_type=F32)


def active(way, step, part, half):
    if step < half:
        return True
    return (part < PARTS // 2) == (way == 0)


def kernel(
    n_rep, n_ep, units, count,
    routes_ref, gates_ref, tok_ref, wg_ref, wu_ref, dir_ref,
    out_ref, scale_ref, ray_ref,
    wcat, cur0, cur1, rows, rgbuf, hid, hid_t, table, table_t,
    rates, part, swap, snd, rcv, picks, arr,
    red_own, red_z, red_psrc, red_p,
    load_sem, rg_sem, row_sem, pair_sem, sib_sem, hid_sem, swap_sem, a2a_sem, back_sem, fwd_sem,
    rz_sem, rp_sem, near_sem,
):
    z = lax.axis_index("rep")
    ep = lax.axis_index("ep")
    chips = n_ep // 2
    per_expert = chips // EXPERTS
    chip, core = ep // 2, lax.rem(ep, 2)
    expert = chip // per_expert
    half = n_rep // 2
    slots = n_rep * CAP
    tok = tok_ref.shape[0]
    width = tok_ref.shape[1] // 2
    third = width // 3 // LANES * LANES
    parity = lax.rem(chip, 2)
    hpiece = slots // PARTS
    tile = min(256, slots)
    tiles = slots // tile
    sib = {"ep": chip * 2 + 1 - core}
    pair = {"ep": (chip + 1 - 2 * parity) * 2 + core}
    own_lanes = pl.ds(pl.multiple_of(core * LANES, LANES), LANES)
    other_lanes = pl.ds(pl.multiple_of((1 - core) * LANES, LANES), LANES)

    def remote(src, dst, sems, index, arrive, device):
        return pltpu.make_async_remote_copy(
            src_ref=src, dst_ref=dst,
            send_sem=sems.at[(0, *index)], recv_sem=sems.at[(1, *arrive)],
            device_id=device, device_id_type=pl.DeviceIdType.MESH,
        )

    side = math.isqrt(chips)
    at_y, at_x = chip // side, lax.rem(chip, side)
    nearby = [
        {"ep": (at_y * side + lax.rem(at_x + d, side)) * 2 + core} for d in (1, side - 1)
    ] + [
        {"ep": (lax.rem(at_y + d, side) * side + at_x) * 2 + core} for d in (1, side - 1)
    ]
    barrier = pltpu.get_barrier_semaphore()

    def signal(sem, device):
        pl.semaphore_signal(
            sem, inc=1, device_id=device, device_id_type=pl.DeviceIdType.MESH
        )

    for device in nearby + [sib] + [{"rep": lax.rem(z + d, n_rep)} for d in (1, n_rep - 1)]:
        signal(barrier, device)

    def greet(r):
        for device in nearby:
            signal(near_sem.at[r], device)

    def met(r):
        pl.semaphore_wait(near_sem.at[r], len(nearby))

    loads = [
        pltpu.make_async_copy(wg_ref, wcat.at[pl.ds(0, units)], load_sem.at[0]),
        pltpu.make_async_copy(wu_ref, wcat.at[pl.ds(LANES, units)], load_sem.at[1]),
        pltpu.make_async_copy(dir_ref, cur0.at[:, pl.ds(0, units)], load_sem.at[2]),
    ]
    for load in loads:
        load.start()
    pad = LANES - units
    wcat[units:LANES, :] = jnp.zeros((pad, wcat.shape[1]), BF16)
    wcat[LANES + units : 2 * LANES, :] = jnp.zeros((pad, wcat.shape[1]), BF16)
    cur0[:, units:LANES, :] = jnp.zeros((n_rep, pad, cur0.shape[2]), BF16)
    hid[:, units:LANES, :] = jnp.zeros((n_rep, pad, slots), BF16)

    before = (
        lax.broadcasted_iota(jnp.int32, (tok, tok), 0)
        < lax.broadcasted_iota(jnp.int32, (tok, tok), 1)
    ).astype(BF16)
    slot_of = lax.broadcasted_iota(jnp.int32, (CAP, tok), 0).astype(F32)

    def slot_table(rg, which):
        hit = jnp.where((rg[0:1] == which) | (rg[1:2] == which), 1.0, 0.0)
        rank = dot(jnp.broadcast_to(hit, (16, tok)).astype(BF16), before)[0:1]
        return jnp.where(slot_of == rank, 1.0, 0.0) * hit

    expert_f = expert.astype(F32)
    own_rg = jnp.concatenate(
        [routes_ref[...].astype(F32), gates_ref[...].astype(F32), jnp.zeros((4, tok), F32)], axis=0
    )
    own_table = slot_table(own_rg, expert_f).astype(BF16)
    rgbuf[z] = own_rg
    step_w = min(512, width)
    for h in range(2):
        for k in range(width // step_w):
            at = h * width + k * step_w
            rows[h, z, :, k * step_w : (k + 1) * step_w] = dot(
                own_table, tok_ref[:, at : at + step_w]
            ).astype(BF16)

    pl.semaphore_wait(barrier, len(nearby) + 3)
    greet(0)

    def block_at(way, step):
        return lax.rem(z + (n_rep - step if way == 0 else step), n_rep)

    def toward(way):
        return {"rep": lax.rem(z + (1 if way == 0 else n_rep - 1), n_rep)}

    def rows_of(q):
        return pl.ds(q % 2 * (CAP // 2), CAP // 2)

    def lanes_of(q):
        if q // 2 == 1:
            return pl.ds(2 * third, width - 2 * third)
        first = parity if q // 2 == 0 else 1 - parity
        return pl.ds(pl.multiple_of(first * third, LANES), third)

    def row_copy(way, step, q):
        ref = rows.at[core, block_at(way, step - 1), rows_of(q), lanes_of(q)]
        i = (way, step - 1, q)
        return remote(ref, ref, row_sem, i, i, toward(way))

    def row_arrival(way, step, q):
        ref = rows.at[core, block_at(way, step), rows_of(q), lanes_of(q)]
        i = (way, step - 1, q)
        return remote(ref, ref, row_sem, i, i, toward(way))

    def pair_copy(way, step, q):
        ref = rows.at[core, block_at(way, step), rows_of(q), lanes_of(q)]
        i = (way, step - 1, q)
        return remote(ref, ref, pair_sem, i, i, pair)

    def pair_arrival(way, step, q):
        ref = rows.at[core, block_at(way, step), rows_of(q), lanes_of(q + 4)]
        i = (way, step - 1, q)
        return remote(ref, ref, pair_sem, i, i, pair)

    def sib_copy(way, step, q):
        ref = rows.at[core, block_at(way, step), rows_of(q), lanes_of(q)]
        i = (way, step - 1, q)
        return remote(ref, ref, sib_sem, i, i, sib)

    def sib_arrival(way, step, q):
        ref = rows.at[1 - core, block_at(way, step), rows_of(q), lanes_of(q)]
        i = (way, step - 1, q)
        return remote(ref, ref, sib_sem, i, i, sib)

    def rg_copy(way, step):
        ref = rgbuf.at[block_at(way, step - 1)]
        i = (way, step - 1)
        return remote(ref, ref, rg_sem, i, i, toward(way))

    def rg_arrival(way, step):
        ref = rgbuf.at[block_at(way, step)]
        i = (way, step - 1)
        return remote(ref, ref, rg_sem, i, i, toward(way))

    order = [
        (step, q, way)
        for step in range(1, half + 1)
        for q in range(PARTS)
        for way in range(2)
        if active(way, step, q, half)
    ]
    passed = [(step, q, way) for step, q, way in order if q < 2]
    whole = [(step, way) for step, q, way in passed if q == 0]
    for way in range(2):
        if active(way, 1, 0, half):
            rg_copy(way, 1).start()
    for step, q, way in order:
        if step == 1:
            row_copy(way, 1, q).start()

    def to_sibling(step, q, way):
        pair_arrival(way, step, q).wait_recv()
        sib_copy(way, step, q + 4).start()

    late = list(passed)
    for step, q, way in order:
        if (q, way) == (0, 0) and 2 <= step <= 4:
            met(step - 2)
            if step < 4:
                greet(step - 1)
        row_arrival(way, step, q).wait_recv()
        if step < half and active(way, step + 1, q, half):
            row_copy(way, step + 1, q).start()
        if q < 2:
            pair_copy(way, step, q).start()
        if q == 0:
            rg_arrival(way, step).wait_recv()
            if step < half and active(way, step + 1, 0, half):
                rg_copy(way, step + 1).start()
        sib_copy(way, step, q).start()
        if q >= 2 and late and late[0][0] < step:
            to_sibling(*late.pop(0))

    for b in range(n_rep):
        rg = rgbuf[b]
        g = jnp.where(rg[0:1] == expert_f, rg[2:3], 0.0) + jnp.where(
            rg[1:2] == expert_f, rg[3:4], 0.0
        )
        rate = jnp.sum(slot_table(rg, expert_f) * g, axis=1, keepdims=True)
        rates[b * CAP : (b + 1) * CAP] = jnp.broadcast_to(rate, (CAP, LANES))
    for load in loads:
        load.wait()
    for step, q, way in late:
        to_sibling(step, q, way)
    for step, q, way in order:
        sib_arrival(way, step, q).wait_recv()
    for step, q, way in passed:
        sib_arrival(way, step, q + 4).wait_recv()

    def hid_copy(way, step, q):
        ref = hid.at[block_at(way, step - 1), pl.ds(0, units), pl.ds(q * hpiece, hpiece)]
        i = (way, step - 1, q)
        return remote(ref, ref, hid_sem, i, i, toward(way))

    def hid_arrival(way, step, q):
        ref = hid.at[block_at(way, step), pl.ds(0, units), pl.ds(q * hpiece, hpiece)]
        i = (way, step - 1, q)
        return remote(ref, ref, hid_sem, i, i, toward(way))

    unit_lanes = pl.ds(pl.multiple_of(z * LANES, LANES), LANES)
    per_tile = tile // CAP
    for m in range(tiles):
        pre = jnp.zeros((tile, 2 * LANES), F32)
        for h in range(2):
            x = rows[h, m * per_tile : (m + 1) * per_tile].reshape(tile, width)
            pre = pre + dot_nt(x, wcat[:, h * width : (h + 1) * width])
        pg, pu = pre[:, :LANES], pre[:, LANES:]
        gated = pg * (1.0 / (1.0 + jnp.exp(-pg))) * pu * rates[m * tile : (m + 1) * tile]
        hid_t[m * tile : (m + 1) * tile, unit_lanes] = gated.astype(BF16)
        hid[z, 0:units, m * tile : (m + 1) * tile] = jnp.transpose(gated, (1, 0))[
            :units
        ].astype(BF16)
        for q in range(m * tile // hpiece, (m + 1) * tile // hpiece):
            for way in range(2):
                if active(way, 1, q, half):
                    hid_copy(way, 1, q).start()

    def own_table_of(e):
        t = slot_table(rgbuf[chip], jnp.float32(e))
        table_t[e * CAP : (e + 1) * CAP, :] = t.astype(BF16)
        tt = jnp.transpose(t, (1, 0))
        table[e] = jnp.concatenate([tt] * per_expert, axis=1).astype(BF16)

    def block_tangent(b, rows_at):
        lanes = pl.ds(pl.multiple_of(b * LANES, LANES), LANES)
        return dot(hid_t[rows_at, lanes], cur0[b])

    for m in range(tiles):
        rows_at = pl.ds(m * tile, tile)
        part[0, rows_at] = block_tangent(z, rows_at)
    for step, q, way in order:
        hid_arrival(way, step, q).wait_recv()
        if step < half and active(way, step + 1, q, half):
            hid_copy(way, step + 1, q).start()
        b = block_at(way, step)
        lanes = pl.ds(pl.multiple_of(b * LANES, LANES), LANES)
        hid_t[q * hpiece : (q + 1) * hpiece, lanes] = jnp.transpose(
            hid[b, :, q * hpiece : (q + 1) * hpiece], (1, 0)
        )
        if step < half:
            rows_at = pl.ds(q * hpiece, hpiece)
            part[0, rows_at] += block_tangent(b, rows_at)
        if q == PARTS - 1 and way == 1:
            for e in range(step - 1, EXPERTS, half):
                own_table_of(e)

    def red_z_copy(it, k):
        b = lax.rem(z + k, n_rep)
        return remote(red_own.at[it], red_z.at[it, z], rz_sem, (it, b), (it, z), {"rep": b})

    def red_z_arrival(it, k):
        b = lax.rem(z + k, n_rep)
        return remote(red_own.at[it], red_z.at[it, b], rz_sem, (it, b), (it, b), {"rep": b})

    def red_p_copy(it, k):
        j = lax.rem(ep + k, n_ep)
        return remote(red_psrc.at[it], red_p.at[it, ep], rp_sem, (it, j), (it, ep), {"ep": j})

    def red_p_arrival(it, k):
        j = lax.rem(ep + k, n_ep)
        return remote(red_psrc.at[it], red_p.at[it, j], rp_sem, (it, j), (it, j), {"ep": j})

    def reduce_z(it):
        red_z[it, z] = red_own[it]

        @pl.loop(1, n_rep)
        def _(k):
            red_z_copy(it, k).start()

    def reduce_plane(it):
        @pl.loop(1, n_rep)
        def _(k):
            red_z_arrival(it, k).wait_recv()

        column = jnp.sum(red_z[it], axis=0)
        red_psrc[it] = column
        red_p[it, ep] = column

        @pl.loop(1, n_ep)
        def _(k):
            red_p_copy(it, k).start()

    def reduce_end(it):
        @pl.loop(1, n_ep)
        def _(k):
            red_p_arrival(it, k).wait_recv()

        return jnp.sum(jnp.sum(red_p[it], axis=0), axis=1, keepdims=True)

    row_y, row_x = chip // per_tile, lax.rem(chip, per_tile)

    def tile_at(i):
        return lax.rem(row_y + i, tiles)

    def swap_copy(it, i):
        at = pl.ds(pl.multiple_of(tile_at(i) * tile, tile), tile)
        return remote(
            part.at[it, at, other_lanes], swap.at[it, at], swap_sem, (it, i), (it, i), sib
        )

    def a2a_copy(it, j):
        return remote(
            snd.at[it, j], rcv.at[it, chip], a2a_sem, (it, j), (it, chip),
            {"ep": j * 2 + core},
        )

    def a2a_arrival(it, k):
        j = lax.rem(chip + k, chips)
        return remote(
            snd.at[it, j], rcv.at[it, j], a2a_sem, (it, j), (it, j), {"ep": j * 2 + core}
        )

    def slot_rows(j):
        return pl.ds(pl.multiple_of(j * CAP, CAP), CAP)

    def back_copy(it, k):
        j = lax.rem(chip + k, chips)
        return remote(
            picks.at[it, j // per_expert], arr.at[it, slot_rows(chip), own_lanes],
            back_sem, (it, j), (it, chip), {"ep": j * 2 + core},
        )

    def back_arrival(it, k):
        j = lax.rem(chip + k, chips)
        return remote(
            picks.at[it, j // per_expert], arr.at[it, slot_rows(j), own_lanes],
            back_sem, (it, j), (it, j), {"ep": j * 2 + core},
        )

    def fwd_copy(it, k):
        j = lax.rem(chip + k, chips)
        ref = arr.at[it, slot_rows(j), own_lanes]
        return remote(ref, ref, fwd_sem, (it, j), (it, j), sib)

    def fwd_arrival(it, k):
        j = lax.rem(chip + k, chips)
        ref = arr.at[it, slot_rows(j), other_lanes]
        return remote(ref, ref, fwd_sem, (it, j), (it, j), sib)

    groups = n_rep * LANES // 256
    columns = cur0.shape[2]

    def fold(v):
        s = jnp.sum(v.reshape(v.shape[0] // 8, 8, columns), axis=0)
        return s[:, :LANES] + s[:, LANES:]

    scale = None
    for it in range(ITERS):
        for i in range(tiles):
            at = pl.ds(pl.multiple_of(tile_at(i) * tile, tile), tile)
            if it == 0:
                part[0, at] += block_tangent(block_at(0, half), at)
            else:
                part[it, at, :] = dot(
                    hid_t[at, :], cur1[...].reshape(n_rep * LANES, columns)
                )
            swap_copy(it, i).start()
        for i in range(tiles):
            swap_copy(it, i).wait_recv()
            m = tile_at(i)
            at = pl.ds(pl.multiple_of(m * tile, tile), tile)
            own = (part[it, at, own_lanes] + swap[it, at]).astype(BF16)
            snd[it, pl.ds(m * per_tile, per_tile)] = own.reshape(per_tile, CAP, LANES)
            if i == 0:
                rcv[it, chip] = snd[it, chip]
            for k in range(1 if i == 0 else 0, per_tile):
                a2a_copy(it, m * per_tile + lax.rem(row_x + k, per_tile)).start()

        @pl.loop(1, chips)
        def _(k):
            a2a_arrival(it, k).wait_recv()

        tangent = jnp.zeros((tok, LANES), F32)
        for e in range(EXPERTS):
            got = rcv[it, e * per_expert : (e + 1) * per_expert].reshape(
                per_expert * CAP, LANES
            )
            tangent = tangent + dot(table[e], got)
        sent = tangent.astype(BF16)
        picks[it] = dot(table_t[...], sent).astype(BF16).reshape(EXPERTS, CAP, LANES)
        arr[it, slot_rows(chip), own_lanes] = picks[it, expert]
        fwd_copy(it, 0).start()

        @pl.loop(1, chips)
        def _(k):
            back_copy(it, k).start()

        if it == 1:
            reduce_plane(0)

        @pl.loop(1, chips)
        def _(k):
            back_arrival(it, k).wait_recv()
            fwd_copy(it, k).start()

        rest = 1.0 / n_rep
        if it == 1:
            scale = lax.rsqrt(reduce_end(0)[0:1] / count + 1e-06)
            power = jnp.exp2(jnp.floor(jnp.log2(scale))).astype(BF16)
            rest = scale / power.astype(F32) * rest

        @pl.loop(0, chips)
        def _(k):
            fwd_arrival(it, k).wait_recv()

        moved = arr[it] if it == 0 else arr[it] * power
        energy = jnp.zeros((8, LANES), F32)
        cross, square = energy, energy
        for g in range(groups):
            x = hid[2 * g : 2 * g + 2].reshape(256, slots)
            p = dot(x, moved) * rest
            energy = energy + fold(p * p)
            if it == 0:
                cur1[2 * g : 2 * g + 2] = p.astype(BF16).reshape(2, LANES, columns)
            else:
                out_ref[2 * g : 2 * g + 2] = p.reshape(2, LANES, columns)[:, :units]
                c = cur1[2 * g : 2 * g + 2].reshape(256, columns).astype(F32) * scale
                cross = cross + fold(c * p)
                square = square + fold(c * c)
        red_own[it] = jnp.concatenate(
            [jnp.sum(v, axis=0, keepdims=True) for v in (energy, cross, square)]
            + [jnp.zeros((5, LANES), F32)],
            axis=0,
        )
        reduce_z(it)

    reduce_plane(1)
    total = reduce_end(1)
    ray = total[1:2] / count / (total[2:3] / count + 1e-06)
    ray_ref[0] = jnp.sum(ray)
    scale_ref[0] = jnp.sum(lax.rsqrt(total[0:1] / count + 1e-06))

    @pl.loop(1, n_rep)
    def _(k):
        for it in range(ITERS):
            red_z_copy(it, k).wait_send()

    for step, q, way in order:
        row_copy(way, step, q).wait_send()
        sib_copy(way, step, q).wait_send()
        hid_copy(way, step, q).wait_send()
    for step, way in whole:
        rg_copy(way, step).wait_send()
    for step, q, way in passed:
        pair_copy(way, step, q).wait_send()
        sib_copy(way, step, q + 4).wait_send()
    for it in range(ITERS):
        for i in range(tiles):
            swap_copy(it, i).wait_send()

        @pl.loop(1, chips)
        def _(k):
            a2a_copy(it, lax.rem(chip + k, chips)).wait_send()
            back_copy(it, k).wait_send()

        @pl.loop(1, n_ep)
        def _(k):
            red_p_copy(it, k).wait_send()

        @pl.loop(0, chips)
        def _(k):
            fwd_copy(it, k).wait_send()


def on_device(tokens, routes, gates, w_gate, w_up, direction):
    n_rep = lax.axis_size("rep")
    n_ep = lax.axis_size("ep")
    chips = n_ep // 2
    tok, depth = tokens.shape
    units, inner = w_gate.shape[1], direction.shape[1]
    columns = direction.shape[2]
    slots = n_rep * CAP
    half = n_rep // 2
    width = depth // 2
    count = float(n_rep * n_ep * inner * columns)
    dma = pltpu.SemaphoreType.DMA
    per_expert = chips // EXPERTS
    out, scale, ray = pl.pallas_call(
        functools.partial(kernel, n_rep, n_ep, units, count),
        out_shape=(
            jax.ShapeDtypeStruct((n_rep, units, columns), F32),
            jax.ShapeDtypeStruct((1,), F32),
            jax.ShapeDtypeStruct((1,), F32),
        ),
        in_specs=[
            pl.BlockSpec(memory_space=pltpu.VMEM),
            pl.BlockSpec(memory_space=pltpu.VMEM),
            pl.BlockSpec(memory_space=pltpu.VMEM),
            pl.BlockSpec(memory_space=pl.ANY),
            pl.BlockSpec(memory_space=pl.ANY),
            pl.BlockSpec(memory_space=pl.ANY),
        ],
        out_specs=(
            pl.BlockSpec(memory_space=pltpu.VMEM),
            pl.BlockSpec(memory_space=pltpu.SMEM),
            pl.BlockSpec(memory_space=pltpu.SMEM),
        ),
        scratch_shapes=[
            pltpu.VMEM((2 * LANES, depth), BF16),
            pltpu.VMEM((n_rep, LANES, columns), BF16),
            pltpu.VMEM((n_rep, LANES, columns), BF16),
            pltpu.VMEM((2, n_rep, CAP, width), BF16),
            pltpu.VMEM((n_rep, 8, tok), F32),
            pltpu.VMEM((n_rep, LANES, slots), BF16),
            pltpu.VMEM((slots, n_rep * LANES), BF16),
            pltpu.VMEM((EXPERTS, tok, per_expert * CAP), BF16),
            pltpu.VMEM((EXPERTS * CAP, tok), BF16),
            pltpu.VMEM((slots, LANES), F32),
            pltpu.VMEM((ITERS, slots, columns), F32),
            pltpu.VMEM((ITERS, slots, LANES), F32),
            pltpu.VMEM((ITERS, chips, CAP, LANES), BF16),
            pltpu.VMEM((ITERS, chips, CAP, LANES), BF16),
            pltpu.VMEM((ITERS, EXPERTS, CAP, LANES), BF16),
            pltpu.VMEM((ITERS, slots, columns), BF16),
            pltpu.VMEM((ITERS, 8, LANES), F32),
            pltpu.VMEM((ITERS, n_rep, 8, LANES), F32),
            pltpu.VMEM((ITERS, 8, LANES), F32),
            pltpu.VMEM((ITERS, n_ep, 8, LANES), F32),
            dma((3,)),
            dma((2, 2, half)),
            dma((2, 2, half, PARTS)),
            dma((2, 2, half, 2)),
            dma((2, 2, half, PARTS + 2)),
            dma((2, 2, half, PARTS)),
            dma((2, ITERS, max(1, slots // 256))),
            dma((2, ITERS, chips)),
            dma((2, ITERS, chips)),
            dma((2, ITERS, chips)),
            dma((2, ITERS, n_rep)),
            dma((2, ITERS, n_ep)),
            pltpu.SemaphoreType.REGULAR((3,)),
        ],
        compiler_params=pltpu.CompilerParams(
            collective_id=0, has_side_effects=True, vmem_limit_bytes=56 * 2**20
        ),
    )(routes.T, gates.T, tokens, w_gate[0], w_up[0], direction[0].reshape(n_rep, units, columns))
    return (out * scale[0]).astype(BF16).reshape(1, inner, columns), ray


def solution(mesh):
    return jax.shard_map(
        on_device,
        mesh=mesh,
        in_specs=(
            P("rep", None),
            P("rep", None),
            P("rep", None),
            P("ep", "rep", None),
            P("ep", "rep", None),
            P("ep", None, "rep"),
        ),
        out_specs=(P("ep", None, "rep"), P()),
        check_vma=False,
    )
```

```python
import functools
import math

import jax
import jax.numpy as jnp
from jax import lax
from jax.experimental import pallas as pl
from jax.experimental.pallas import tpu as pltpu
from jax.sharding import PartitionSpec as P

EXPERTS = 8
CAP = 64
ITERS = 2
LANES = 128
PARTS = 4
F32, BF16 = jnp.float32, jnp.bfloat16


def dot(a, b):
    return jnp.dot(a, b, preferred_element_type=F32)


def dot_nt(a, b):
    return lax.dot_general(a, b, (((1,), (1,)), ((), ())), preferred_element_type=F32)


def active(way, step, part, half):
    if step < half:
        return True
    return (part < PARTS // 2) == (way == 0)


def kernel(
    n_rep, n_ep, units, count,
    routes_ref, gates_ref, tok_hbm, wg_ref, wu_ref, dir_ref,
    out_hbm, scale_ref, ray_ref,
    wcat, cur0, gram, tang, rows, rgbuf, hid, hid_t, table, table_t,
    rates, part, swap, snd, rcv, picks, arr, tok_ref, out_ref,
    red_own, red_z, red_psrc, red_p,
    load_sem, rg_sem, row_sem, pair_sem, sib_sem, hid_sem, swap_sem, a2a_sem, back_sem, fwd_sem,
    rz_sem, rp_sem, near_sem,
):
    z = lax.axis_index("rep")
    ep = lax.axis_index("ep")
    chips = n_ep // 2
    per_expert = chips // EXPERTS
    chip, core = ep // 2, lax.rem(ep, 2)
    expert = chip // per_expert
    half = n_rep // 2
    slots = n_rep * CAP
    tok = tok_ref.shape[0]
    width = tok_ref.shape[1] // 2
    third = width // 3 // LANES * LANES
    parity = lax.rem(chip, 2)
    hpiece = slots // PARTS
    tile = min(256, slots)
    tiles = slots // tile
    sib = {"ep": chip * 2 + 1 - core}
    pair = {"ep": (chip + 1 - 2 * parity) * 2 + core}
    own_lanes = pl.ds(pl.multiple_of(core * LANES, LANES), LANES)
    other_lanes = pl.ds(pl.multiple_of((1 - core) * LANES, LANES), LANES)

    def remote(src, dst, sems, index, arrive, device):
        return pltpu.make_async_remote_copy(
            src_ref=src, dst_ref=dst,
            send_sem=sems.at[(0, *index)], recv_sem=sems.at[(1, *arrive)],
            device_id=device, device_id_type=pl.DeviceIdType.MESH,
        )

    side = math.isqrt(chips)
    at_y, at_x = chip // side, lax.rem(chip, side)
    nearby = [
        {"ep": (at_y * side + lax.rem(at_x + d, side)) * 2 + core} for d in (1, side - 1)
    ] + [
        {"ep": (lax.rem(at_y + d, side) * side + at_x) * 2 + core} for d in (1, side - 1)
    ]
    barrier = pltpu.get_barrier_semaphore()

    def signal(sem, device):
        pl.semaphore_signal(
            sem, inc=1, device_id=device, device_id_type=pl.DeviceIdType.MESH
        )

    for device in nearby + [sib] + [{"rep": lax.rem(z + d, n_rep)} for d in (1, n_rep - 1)]:
        signal(barrier, device)

    def greet(r):
        for device in nearby:
            signal(near_sem.at[r], device)

    def met(r):
        pl.semaphore_wait(near_sem.at[r], len(nearby))

    loads = [
        pltpu.make_async_copy(wg_ref, wcat.at[pl.ds(0, units)], load_sem.at[0]),
        pltpu.make_async_copy(wu_ref, wcat.at[pl.ds(LANES, units)], load_sem.at[1]),
        pltpu.make_async_copy(dir_ref, cur0.at[:, pl.ds(0, units)], load_sem.at[2]),
    ]
    load_tokens = pltpu.make_async_copy(tok_hbm, tok_ref, load_sem.at[3])
    load_tokens.start()
    for load in loads:
        load.start()
    pad = LANES - units
    wcat[units:LANES, :] = jnp.zeros((pad, wcat.shape[1]), BF16)
    wcat[LANES + units : 2 * LANES, :] = jnp.zeros((pad, wcat.shape[1]), BF16)
    cur0[:, units:LANES, :] = jnp.zeros((n_rep, pad, cur0.shape[2]), BF16)
    hid[:, units:LANES, :] = jnp.zeros((n_rep, pad, slots), BF16)

    before = (
        lax.broadcasted_iota(jnp.int32, (tok, tok), 0)
        < lax.broadcasted_iota(jnp.int32, (tok, tok), 1)
    ).astype(BF16)
    slot_of = lax.broadcasted_iota(jnp.int32, (CAP, tok), 0).astype(F32)

    def slot_table(rg, which):
        hit = jnp.where((rg[0:1] == which) | (rg[1:2] == which), 1.0, 0.0)
        rank = dot(jnp.broadcast_to(hit, (16, tok)).astype(BF16), before)[0:1]
        return jnp.where(slot_of == rank, 1.0, 0.0) * hit

    expert_f = expert.astype(F32)
    own_rg = jnp.concatenate(
        [routes_ref[...].astype(F32), gates_ref[...].astype(F32), jnp.zeros((4, tok), F32)], axis=0
    )
    own_table = slot_table(own_rg, expert_f).astype(BF16)
    rgbuf[z] = own_rg
    load_tokens.wait()
    step_w = min(512, width)
    for h in range(2):
        for k in range(width // step_w):
            at = h * width + k * step_w
            rows[h, z, :, k * step_w : (k + 1) * step_w] = dot(
                own_table, tok_ref[:, at : at + step_w]
            ).astype(BF16)

    pl.semaphore_wait(barrier, len(nearby) + 3)
    greet(0)

    def block_at(way, step):
        return lax.rem(z + (n_rep - step if way == 0 else step), n_rep)

    def toward(way):
        return {"rep": lax.rem(z + (1 if way == 0 else n_rep - 1), n_rep)}

    def rows_of(q):
        return pl.ds(q % 2 * (CAP // 2), CAP // 2)

    def lanes_of(q):
        if q // 2 == 1:
            return pl.ds(2 * third, width - 2 * third)
        first = parity if q // 2 == 0 else 1 - parity
        return pl.ds(pl.multiple_of(first * third, LANES), third)

    def row_copy(way, step, q):
        ref = rows.at[core, block_at(way, step - 1), rows_of(q), lanes_of(q)]
        i = (way, step - 1, q)
        return remote(ref, ref, row_sem, i, i, toward(way))

    def row_arrival(way, step, q):
        ref = rows.at[core, block_at(way, step), rows_of(q), lanes_of(q)]
        i = (way, step - 1, q)
        return remote(ref, ref, row_sem, i, i, toward(way))

    def pair_copy(way, step, q):
        ref = rows.at[core, block_at(way, step), rows_of(q), lanes_of(q)]
        i = (way, step - 1, q)
        return remote(ref, ref, pair_sem, i, i, pair)

    def pair_arrival(way, step, q):
        ref = rows.at[core, block_at(way, step), rows_of(q), lanes_of(q + 4)]
        i = (way, step - 1, q)
        return remote(ref, ref, pair_sem, i, i, pair)

    def sib_copy(way, step, q):
        ref = rows.at[core, block_at(way, step), rows_of(q), lanes_of(q)]
        i = (way, step - 1, q)
        return remote(ref, ref, sib_sem, i, i, sib)

    def sib_arrival(way, step, q):
        ref = rows.at[1 - core, block_at(way, step), rows_of(q), lanes_of(q)]
        i = (way, step - 1, q)
        return remote(ref, ref, sib_sem, i, i, sib)

    def rg_copy(way, step):
        ref = rgbuf.at[block_at(way, step - 1)]
        i = (way, step - 1)
        return remote(ref, ref, rg_sem, i, i, toward(way))

    def rg_arrival(way, step):
        ref = rgbuf.at[block_at(way, step)]
        i = (way, step - 1)
        return remote(ref, ref, rg_sem, i, i, toward(way))

    order = [
        (step, q, way)
        for step in range(1, half + 1)
        for q in range(PARTS)
        for way in range(2)
        if active(way, step, q, half)
    ]
    passed = [(step, q, way) for step, q, way in order if q < 2]
    whole = [(step, way) for step, q, way in passed if q == 0]
    for way in range(2):
        if active(way, 1, 0, half):
            rg_copy(way, 1).start()
    for step, q, way in order:
        if step == 1:
            row_copy(way, 1, q).start()

    def to_sibling(step, q, way):
        pair_arrival(way, step, q).wait_recv()
        sib_copy(way, step, q + 4).start()

    late = list(passed)
    for step, q, way in order:
        if (q, way) == (0, 0) and 2 <= step <= 4:
            met(step - 2)
            if step < 4:
                greet(step - 1)
        row_arrival(way, step, q).wait_recv()
        if step < half and active(way, step + 1, q, half):
            row_copy(way, step + 1, q).start()
        if q < 2:
            pair_copy(way, step, q).start()
        if q == 0:
            rg_arrival(way, step).wait_recv()
            if step < half and active(way, step + 1, 0, half):
                rg_copy(way, step + 1).start()
        sib_copy(way, step, q).start()
        if q >= 2 and late and late[0][0] < step:
            to_sibling(*late.pop(0))

    for b in range(n_rep):
        rg = rgbuf[b]
        g = jnp.where(rg[0:1] == expert_f, rg[2:3], 0.0) + jnp.where(
            rg[1:2] == expert_f, rg[3:4], 0.0
        )
        rate = jnp.sum(slot_table(rg, expert_f) * g, axis=1, keepdims=True)
        rates[b * CAP : (b + 1) * CAP] = jnp.broadcast_to(rate, (CAP, LANES))
    for load in loads:
        load.wait()
    for step, q, way in late:
        to_sibling(step, q, way)
    for step, q, way in order:
        sib_arrival(way, step, q).wait_recv()
    for step, q, way in passed:
        sib_arrival(way, step, q + 4).wait_recv()

    def hid_copy(way, step, q):
        ref = hid.at[block_at(way, step - 1), pl.ds(0, units), pl.ds(q * hpiece, hpiece)]
        i = (way, step - 1, q)
        return remote(ref, ref, hid_sem, i, i, toward(way))

    def hid_arrival(way, step, q):
        ref = hid.at[block_at(way, step), pl.ds(0, units), pl.ds(q * hpiece, hpiece)]
        i = (way, step - 1, q)
        return remote(ref, ref, hid_sem, i, i, toward(way))

    unit_lanes = pl.ds(pl.multiple_of(z * LANES, LANES), LANES)
    per_tile = tile // CAP
    for m in range(tiles):
        pre = jnp.zeros((tile, 2 * LANES), F32)
        for h in range(2):
            x = rows[h, m * per_tile : (m + 1) * per_tile].reshape(tile, width)
            pre = pre + dot_nt(x, wcat[:, h * width : (h + 1) * width])
        pg, pu = pre[:, :LANES], pre[:, LANES:]
        gated = pg * (1.0 / (1.0 + jnp.exp(-pg))) * pu * rates[m * tile : (m + 1) * tile]
        hid_t[m * tile : (m + 1) * tile, unit_lanes] = gated.astype(BF16)
        hid[z, 0:units, m * tile : (m + 1) * tile] = jnp.transpose(gated, (1, 0))[
            :units
        ].astype(BF16)
        for q in range(m * tile // hpiece, (m + 1) * tile // hpiece):
            for way in range(2):
                if active(way, 1, q, half):
                    hid_copy(way, 1, q).start()

    def own_table_of(e):
        t = slot_table(rgbuf[chip], jnp.float32(e))
        table_t[e * CAP : (e + 1) * CAP, :] = t.astype(BF16)
        tt = jnp.transpose(t, (1, 0))
        table[e] = jnp.concatenate([tt] * per_expert, axis=1).astype(BF16)

    def block_tangent(b, rows_at):
        lanes = pl.ds(pl.multiple_of(b * LANES, LANES), LANES)
        return dot(hid_t[rows_at, lanes], cur0[b])

    for m in range(tiles):
        rows_at = pl.ds(m * tile, tile)
        part[0, rows_at] = block_tangent(z, rows_at)
    for step, q, way in order:
        hid_arrival(way, step, q).wait_recv()
        if step < half and active(way, step + 1, q, half):
            hid_copy(way, step + 1, q).start()
        b = block_at(way, step)
        lanes = pl.ds(pl.multiple_of(b * LANES, LANES), LANES)
        hid_t[q * hpiece : (q + 1) * hpiece, lanes] = jnp.transpose(
            hid[b, :, q * hpiece : (q + 1) * hpiece], (1, 0)
        )
        if step < half:
            rows_at = pl.ds(q * hpiece, hpiece)
            part[0, rows_at] += block_tangent(b, rows_at)
        if q == PARTS - 1 and way == 1:
            for e in range(step - 1, EXPERTS, half):
                own_table_of(e)

    def red_z_copy(it, k):
        b = lax.rem(z + k, n_rep)
        return remote(red_own.at[it], red_z.at[it, z], rz_sem, (it, b), (it, z), {"rep": b})

    def red_z_arrival(it, k):
        b = lax.rem(z + k, n_rep)
        return remote(red_own.at[it], red_z.at[it, b], rz_sem, (it, b), (it, b), {"rep": b})

    def red_p_copy(it, k):
        j = lax.rem(ep + k, n_ep)
        return remote(red_psrc.at[it], red_p.at[it, ep], rp_sem, (it, j), (it, ep), {"ep": j})

    def red_p_arrival(it, k):
        j = lax.rem(ep + k, n_ep)
        return remote(red_psrc.at[it], red_p.at[it, j], rp_sem, (it, j), (it, j), {"ep": j})

    def reduce_z(it):
        red_z[it, z] = red_own[it]

        @pl.loop(1, n_rep)
        def _(k):
            red_z_copy(it, k).start()

    def reduce_plane(it):
        @pl.loop(1, n_rep)
        def _(k):
            red_z_arrival(it, k).wait_recv()

        column = jnp.sum(red_z[it], axis=0)
        red_psrc[it] = column
        red_p[it, ep] = column

        @pl.loop(1, n_ep)
        def _(k):
            red_p_copy(it, k).start()

    def reduce_end(it):
        @pl.loop(1, n_ep)
        def _(k):
            red_p_arrival(it, k).wait_recv()

        return jnp.sum(jnp.sum(red_p[it], axis=0), axis=1, keepdims=True)

    row_y, row_x = chip // per_tile, lax.rem(chip, per_tile)

    def tile_at(i):
        return lax.rem(row_y + i, tiles)

    def swap_copy(it, i):
        at = pl.ds(pl.multiple_of(tile_at(i) * tile, tile), tile)
        return remote(
            part.at[it, at, other_lanes], swap.at[it, at], swap_sem, (it, i), (it, i), sib
        )

    def a2a_copy(it, j):
        return remote(
            snd.at[it, j], rcv.at[it, chip], a2a_sem, (it, j), (it, chip),
            {"ep": j * 2 + core},
        )

    def a2a_arrival(it, k):
        j = lax.rem(chip + k, chips)
        return remote(
            snd.at[it, j], rcv.at[it, j], a2a_sem, (it, j), (it, j), {"ep": j * 2 + core}
        )

    def slot_rows(j):
        return pl.ds(pl.multiple_of(j * CAP, CAP), CAP)

    def back_copy(it, k):
        j = lax.rem(chip + k, chips)
        return remote(
            picks.at[it, j // per_expert], arr.at[it, slot_rows(chip), own_lanes],
            back_sem, (it, j), (it, chip), {"ep": j * 2 + core},
        )

    def back_arrival(it, k):
        j = lax.rem(chip + k, chips)
        return remote(
            picks.at[it, j // per_expert], arr.at[it, slot_rows(j), own_lanes],
            back_sem, (it, j), (it, j), {"ep": j * 2 + core},
        )

    def fwd_copy(it, k):
        j = lax.rem(chip + k, chips)
        ref = arr.at[it, slot_rows(j), own_lanes]
        return remote(ref, ref, fwd_sem, (it, j), (it, j), sib)

    def fwd_arrival(it, k):
        j = lax.rem(chip + k, chips)
        ref = arr.at[it, slot_rows(j), other_lanes]
        return remote(ref, ref, fwd_sem, (it, j), (it, j), sib)

    groups = n_rep * LANES // 256
    columns = cur0.shape[2]

    def fold(v):
        s = jnp.sum(v.reshape(v.shape[0] // 8, 8, columns), axis=0)
        return s[:, :LANES] + s[:, LANES:]

    def gram_tile(r):
        at = slice(r * tile, (r + 1) * tile)
        g = dot(hid_t[at], hid[...].reshape(n_rep * LANES, slots))
        high = g.astype(BF16)
        gram[0, at] = high
        gram[1, at] = (g - high.astype(F32)).astype(BF16)

    def lane_sum(v):
        return jnp.sum(v, axis=0, keepdims=True)

    first = max(1, tiles // 2)
    scale = None
    for it in range(ITERS):
        energy = jnp.zeros((8, LANES), F32)
        for i in range(tiles):
            at = pl.ds(pl.multiple_of(tile_at(i) * tile, tile), tile)
            if it == 0:
                part[0, at] += block_tangent(block_at(0, half), at)
            else:
                back = (dot(gram[0, at], arr[0]) + dot(gram[1, at], arr[0])) / n_rep
                part[it, at, :] = back
                energy = energy + fold(back * arr[0, at].astype(F32)) / n_rep
            swap_copy(it, i).start()
        if it == 1:
            red_own[0] = jnp.concatenate(
                [lane_sum(energy), jnp.zeros((7, LANES), F32)], axis=0
            )
            reduce_z(0)
        for i in range(tiles):
            swap_copy(it, i).wait_recv()
            m = tile_at(i)
            at = pl.ds(pl.multiple_of(m * tile, tile), tile)
            own = (part[it, at, own_lanes] + swap[it, at]).astype(BF16)
            snd[it, pl.ds(m * per_tile, per_tile)] = own.reshape(per_tile, CAP, LANES)
            if i == 0:
                rcv[it, chip] = snd[it, chip]
            for k in range(1 if i == 0 else 0, per_tile):
                a2a_copy(it, m * per_tile + lax.rem(row_x + k, per_tile)).start()

        if it == 0:
            for r in range(first):
                gram_tile(r)

        @pl.loop(1, chips)
        def _(k):
            a2a_arrival(it, k).wait_recv()

        tangent = jnp.zeros((tok, LANES), F32)
        for e in range(EXPERTS):
            got = rcv[it, e * per_expert : (e + 1) * per_expert].reshape(
                per_expert * CAP, LANES
            )
            tangent = tangent + dot(table[e], got)
        if it == 1:
            tang[...] = tangent
        sent = tangent.astype(BF16)
        picks[it] = dot(table_t[...], sent).astype(BF16).reshape(EXPERTS, CAP, LANES)
        arr[it, slot_rows(chip), own_lanes] = picks[it, expert]
        fwd_copy(it, 0).start()

        @pl.loop(1, chips)
        def _(k):
            back_copy(it, k).start()

        if it == 0:
            for r in range(first, tiles):
                gram_tile(r)
        else:
            reduce_plane(0)

        @pl.loop(1, chips)
        def _(k):
            back_arrival(it, k).wait_recv()
            fwd_copy(it, k).start()

        if it == 1:
            mean = jnp.maximum(reduce_end(0)[0:1], 0.0) / count
            scale = lax.rsqrt(mean + 1e-06)
            power = jnp.exp2(jnp.floor(jnp.log2(scale))).astype(BF16)
            rest = scale / power.astype(F32) / n_rep
            t = tang[...] * scale
            cross = lane_sum(t * (tang[...].astype(BF16).astype(F32) * scale)) / n_rep

        @pl.loop(0, chips)
        def _(k):
            fwd_arrival(it, k).wait_recv()

    moved = arr[1] * power
    energy = jnp.zeros((8, LANES), F32)
    for g in range(groups):
        x = hid[2 * g : 2 * g + 2].reshape(256, slots)
        p = dot(x, moved) * rest
        energy = energy + fold(p * p)
        out_ref[2 * g : 2 * g + 2] = p.reshape(2, LANES, columns)[:, :units]
    red_own[1] = jnp.concatenate(
        [lane_sum(energy), cross, jnp.zeros((6, LANES), F32)], axis=0
    )
    reduce_z(1)
    store = pltpu.make_async_copy(out_ref, out_hbm, load_sem.at[4])
    store.start()
    reduce_plane(1)
    total = reduce_end(1)
    store.wait()
    ray = total[1:2] / count / (scale * scale * mean + 1e-06)
    ray_ref[0] = jnp.sum(ray)
    scale_ref[0] = jnp.sum(lax.rsqrt(total[0:1] / count + 1e-06))

    @pl.loop(1, n_rep)
    def _(k):
        for it in range(ITERS):
            red_z_copy(it, k).wait_send()

    for step, q, way in order:
        row_copy(way, step, q).wait_send()
        sib_copy(way, step, q).wait_send()
        hid_copy(way, step, q).wait_send()
    for step, way in whole:
        rg_copy(way, step).wait_send()
    for step, q, way in passed:
        pair_copy(way, step, q).wait_send()
        sib_copy(way, step, q + 4).wait_send()
    for it in range(ITERS):
        for i in range(tiles):
            swap_copy(it, i).wait_send()

        @pl.loop(1, chips)
        def _(k):
            a2a_copy(it, lax.rem(chip + k, chips)).wait_send()
            back_copy(it, k).wait_send()

        @pl.loop(1, n_ep)
        def _(k):
            red_p_copy(it, k).wait_send()

        @pl.loop(0, chips)
        def _(k):
            fwd_copy(it, k).wait_send()


def on_device(tokens, routes, gates, w_gate, w_up, direction):
    n_rep = lax.axis_size("rep")
    n_ep = lax.axis_size("ep")
    chips = n_ep // 2
    tok, depth = tokens.shape
    units, inner = w_gate.shape[1], direction.shape[1]
    columns = direction.shape[2]
    slots = n_rep * CAP
    half = n_rep // 2
    width = depth // 2
    count = float(n_rep * n_ep * inner * columns)
    dma = pltpu.SemaphoreType.DMA
    per_expert = chips // EXPERTS
    out, scale, ray = pl.pallas_call(
        functools.partial(kernel, n_rep, n_ep, units, count),
        out_shape=(
            jax.ShapeDtypeStruct((n_rep, units, columns), F32),
            jax.ShapeDtypeStruct((1,), F32),
            jax.ShapeDtypeStruct((1,), F32),
        ),
        in_specs=[
            pl.BlockSpec(memory_space=pltpu.VMEM),
            pl.BlockSpec(memory_space=pltpu.VMEM),
            pl.BlockSpec(memory_space=pl.ANY),
            pl.BlockSpec(memory_space=pl.ANY),
            pl.BlockSpec(memory_space=pl.ANY),
            pl.BlockSpec(memory_space=pl.ANY),
        ],
        out_specs=(
            pl.BlockSpec(memory_space=pl.ANY),
            pl.BlockSpec(memory_space=pltpu.SMEM),
            pl.BlockSpec(memory_space=pltpu.SMEM),
        ),
        scratch_shapes=[
            pltpu.VMEM((2 * LANES, depth), BF16),
            pltpu.VMEM((n_rep, LANES, columns), BF16),
            pltpu.VMEM((2, slots, slots), BF16),
            pltpu.VMEM((tok, LANES), F32),
            pltpu.VMEM((2, n_rep, CAP, width), BF16),
            pltpu.VMEM((n_rep, 8, tok), F32),
            pltpu.VMEM((n_rep, LANES, slots), BF16),
            pltpu.VMEM((slots, n_rep * LANES), BF16),
            pltpu.VMEM((EXPERTS, tok, per_expert * CAP), BF16),
            pltpu.VMEM((EXPERTS * CAP, tok), BF16),
            pltpu.VMEM((slots, LANES), F32),
            pltpu.VMEM((ITERS, slots, columns), F32),
            pltpu.VMEM((ITERS, slots, LANES), F32),
            pltpu.VMEM((ITERS, chips, CAP, LANES), BF16),
            pltpu.VMEM((ITERS, chips, CAP, LANES), BF16),
            pltpu.VMEM((ITERS, EXPERTS, CAP, LANES), BF16),
            pltpu.VMEM((ITERS, slots, columns), BF16),
            pltpu.VMEM((tok, depth), BF16),
            pltpu.VMEM((n_rep, units, columns), F32),
            pltpu.VMEM((ITERS, 8, LANES), F32),
            pltpu.VMEM((ITERS, n_rep, 8, LANES), F32),
            pltpu.VMEM((ITERS, 8, LANES), F32),
            pltpu.VMEM((ITERS, n_ep, 8, LANES), F32),
            dma((5,)),
            dma((2, 2, half)),
            dma((2, 2, half, PARTS)),
            dma((2, 2, half, 2)),
            dma((2, 2, half, PARTS + 2)),
            dma((2, 2, half, PARTS)),
            dma((2, ITERS, max(1, slots // 256))),
            dma((2, ITERS, chips)),
            dma((2, ITERS, chips)),
            dma((2, ITERS, chips)),
            dma((2, ITERS, n_rep)),
            dma((2, ITERS, n_ep)),
            pltpu.SemaphoreType.REGULAR((3,)),
        ],
        compiler_params=pltpu.CompilerParams(
            collective_id=0, has_side_effects=True, vmem_limit_bytes=56 * 2**20
        ),
    )(routes.T, gates.T, tokens, w_gate[0], w_up[0], direction[0].reshape(n_rep, units, columns))
    return (out * scale[0]).astype(BF16).reshape(1, inner, columns), ray


def solution(mesh):
    return jax.shard_map(
        on_device,
        mesh=mesh,
        in_specs=(
            P("rep", None),
            P("rep", None),
            P("rep", None),
            P("ep", "rep", None),
            P("ep", "rep", None),
            P("ep", None, "rep"),
        ),
        out_specs=(P("ep", None, "rep"), P()),
        check_vma=False,
    )
```
